128 devices in a mesh: tm: 128 (over y, z, x, core).
Axes of the slice: x: 4, y: 4, z: 4, core: 2. Of those that a mesh axis runs over, the one named last changes fastest.
Arguments:
- stream: bfloat16 [262144, 128], P('tm'), may hold values from -160 to 160
- stem_weight: bfloat16 [7, 128, 128], replicated, may hold values from -0.1875 to 0.1875
- stem_bias: float32 [128], replicated, may hold values from -3 to 3
- first_weight: bfloat16 [3, 128, 256], replicated, may hold values from -0.3125 to 0.3125
- deep_weight: bfloat16 [3, 3, 256, 256], replicated, may hold values from -0.21875 to 0.21875
- layer_bias: float32 [4, 256], replicated, may hold values from -3 to 3
- head_weight: bfloat16 [256, 128], replicated, may hold values from -0.375 to 0.375
- head_bias: float32 [128], replicated, may hold values from -3 to 3
- profiles: float32 [4, 4096], replicated, may hold values from 0.25 to 2
- starts: int32 [512], P('tm'), may hold values from 0 to 258048, as said below
- profile_index: int32 [512], P('tm'), may hold values from 0 to 3
- counts: int32 [128], P('tm'), may hold values from 1 to 4, as said below
Outputs:
- embedding: bfloat16 [262144, 128], P('tm')
The draws below stay inside these ranges and needn't reach their ends.
Inputs may be any that keep to these rules, and one draw needn't show every extreme that they name: `starts`: window slot d * 4 + j belongs to index d of tm; its start is a multiple of 256 from max(0, (d - 1) * 2048) to min((d + 1) * 2048 - 256, 258048). Index d of tm has live windows in its first counts[d] slots; some index has all 4.
All inputs are finite; a program needn't handle non-finite values.
Results may differ from the reference program's by a relative error of at most 0.013.
Values may be sent and summed in bfloat16 or wider, within the bound.
A program may use at most 128 MiB of HBM per device.

```python
import math
import jax
import jax.numpy as jnp
from jax import lax

SENS = 128
STEM = 128
HID = 256
KS = 7
KT = 3
LAYERS = 4
WMAX = 4
NPROF = 4
TS = 2048
WL = 4096
SEG = 256
TIME = 262144
WINDOWS = 512
N_TM = 128


def draw_stream(key, part):
    key = jax.random.fold_in(key, 5)
    noise_key, scale_key = jax.random.split(key, 2)
    segment_count = TIME // SEG
    top_log = math.log(10.0)
    noise = jnp.clip(jax.random.normal(noise_key, (TIME, SENS), jnp.float32), -4.0, 4.0)
    segment_scale = jnp.exp(jax.random.uniform(scale_key, (segment_count, 1), jnp.float32, 0.0, top_log))
    row_scale = jnp.repeat(segment_scale, SEG, axis=0)
    ramp = 1.0 + 2.0 * jnp.arange(TIME, dtype=jnp.float32)[:, None] / TIME
    return (noise * row_scale * ramp).astype(jnp.bfloat16)


def draw_starts(key, part):
    key = jax.random.fold_in(key, 11)
    window_ids = jnp.arange(WINDOWS, dtype=jnp.int32)
    owner_rank = window_ids // WMAX
    segment_steps = jax.random.randint(key, (WINDOWS,), 0, 2 * TS // SEG, dtype=jnp.int32)
    raw_starts = (owner_rank - 1) * TS + segment_steps * SEG
    clipped = jnp.clip(raw_starts, 0, TIME - WL)
    clipped = jnp.where(window_ids == 0, 0, clipped)
    clipped = jnp.where(window_ids == WINDOWS - WMAX, TIME - WL, clipped)
    return clipped.astype(jnp.int32)


def draw_counts(key, part):
    key = jax.random.fold_in(key, 23)
    first_key, second_key = jax.random.split(key)
    rolled = jax.random.randint(first_key, (N_TM,), 0, 10, dtype=jnp.int32)
    loaded = jnp.where(rolled < 7, 1, WMAX)
    busiest = jax.random.randint(second_key, (), 0, N_TM, dtype=jnp.int32)
    loaded = jnp.where(jnp.arange(N_TM, dtype=jnp.int32) == busiest, WMAX, loaded)
    return loaded.astype(jnp.int32)


def plant(values, stream_key, low, largest):
    place = [jax.random.randint(jax.random.fold_in(stream_key, axis), (), 0, length) for axis, length in enumerate(values.shape)]
    main_axis = values.shape.index(max(values.shape))
    beside = place[:main_axis] + [(place[main_axis] + 1) % values.shape[main_axis]] + place[main_axis + 1:]
    return values.at[tuple(place)].set(low).at[tuple(beside)].set(largest)


def bell_draw(key, dims, scale, reach, held_as=jnp.bfloat16):
    entries = jax.random.normal(key, dims, jnp.float32) * scale
    return jnp.minimum(jnp.maximum(entries, -reach), reach).astype(held_as)


def setup_inputs(seed: int = 0) -> dict:
    streams_of = jax.random.split(jax.random.key(seed), 13)
    return {
        "stream": draw_stream(jax.random.fold_in(streams_of[12], 71), 0),
        "stem_weight": bell_draw(streams_of[1], (KS, SENS, STEM), (KS * SENS) ** -0.5, 0.1875),
        "stem_bias": bell_draw(streams_of[2], (STEM,), 0.5, 3.0, jnp.float32),
        "first_weight": bell_draw(streams_of[3], (KT, STEM, HID), (KT * STEM) ** -0.5, 0.3125),
        "deep_weight": bell_draw(streams_of[4], (LAYERS - 1, KT, HID, HID), (KT * HID) ** -0.5, 0.21875),
        "layer_bias": bell_draw(streams_of[5], (LAYERS, HID), 0.5, 3.0, jnp.float32),
        "head_weight": bell_draw(streams_of[6], (HID, STEM), HID ** -0.5, 0.375),
        "head_bias": bell_draw(streams_of[7], (STEM,), 0.5, 3.0, jnp.float32),
        "profiles": jnp.clip(jnp.exp(jax.random.uniform(streams_of[8], (NPROF, WL), jnp.float32, math.log(0.25), math.log(2.0))), 0.25, 2.0),
        "starts": draw_starts(jax.random.fold_in(streams_of[12], 71), 0),
        "profile_index": plant(jax.random.randint(streams_of[10], (WINDOWS,), 0, NPROF), jax.random.fold_in(streams_of[10], 1), 0, NPROF - 1).astype(jnp.int32),
        "counts": draw_counts(jax.random.fold_in(streams_of[12], 71), 0),
    }


norm_epsilon = 1e-05

def stem_layer(padded, stem_weight, stem_bias):
    length = padded.shape[0] - stem_weight.shape[0] + 1
    summed = jnp.zeros((length, stem_weight.shape[2]), jnp.float32) + stem_bias
    for k in range(stem_weight.shape[0]):
        summed = summed + jnp.dot(padded[k:k + length], stem_weight[k], preferred_element_type=jnp.float32)
    return jax.nn.gelu(summed).astype(jnp.bfloat16)

def normalize_window(window_rows):
    values = window_rows.astype(jnp.float32)
    mean_value = lax.optimization_barrier(jnp.mean(values, axis=0))
    spread = lax.optimization_barrier(jnp.mean(values * values, axis=0)) - mean_value * mean_value
    return ((values - mean_value) * lax.rsqrt(spread + norm_epsilon)).astype(jnp.bfloat16)

def temporal_net(window_rows, first_weight, deep_weight, layer_bias, head_weight, head_bias):
    length = window_rows.shape[0]
    hidden = window_rows
    for layer_index in range(deep_weight.shape[0] + 1):
        kernel = first_weight if layer_index == 0 else deep_weight[layer_index - 1]
        spread = 2 ** layer_index
        tap_count = kernel.shape[0]
        padded = jnp.pad(hidden, ((spread * (tap_count - 1), 0), (0, 0)))
        summed = jnp.zeros((length, kernel.shape[2]), jnp.float32) + layer_bias[layer_index]
        for k in range(tap_count):
            summed = summed + jnp.dot(padded[k * spread:k * spread + length], kernel[k], preferred_element_type=jnp.float32)
        active = jax.nn.gelu(summed)
        if layer_index > 0:
            active = active + hidden.astype(jnp.float32)
        hidden = active.astype(jnp.bfloat16)
    projected = jnp.dot(hidden, head_weight, preferred_element_type=jnp.float32) + head_bias
    return projected.astype(jnp.bfloat16)

def reference(stream, stem_weight, stem_bias, first_weight, deep_weight, layer_bias, head_weight, head_bias, profiles, starts, profile_index, counts):
    margin = (stem_weight.shape[0] - 1) // 2
    features = stem_layer(jnp.pad(stream, ((margin, margin), (0, 0))), stem_weight, stem_bias)
    window_ids = jnp.arange(WINDOWS, dtype=jnp.int32)
    living_mask = window_ids % WMAX < counts[window_ids // WMAX]
    channels = features.shape[1]
    zero_index = jnp.zeros((), jnp.int32)

    def visit(running, window_item):
        window_start, chosen, living = window_item
        window_start = window_start.astype(jnp.int32)

        def accumulate(totals_now):
            weighted, weight_total = totals_now
            window_rows = lax.dynamic_slice(features, (window_start, zero_index), (WL, channels))
            normed = normalize_window(window_rows)
            output = temporal_net(normed, first_weight, deep_weight, layer_bias, head_weight, head_bias)
            profile_row = profiles[chosen]
            previous = lax.dynamic_slice(weighted, (window_start, zero_index), (WL, channels))
            weighted = lax.dynamic_update_slice(weighted, previous + output.astype(jnp.float32) * profile_row[:, None], (window_start, zero_index))
            previous_total = lax.dynamic_slice(weight_total, (window_start,), (WL,))
            weight_total = lax.dynamic_update_slice(weight_total, previous_total + profile_row, (window_start,))
            return (weighted, weight_total)

        def unchanged(totals_now):
            return totals_now
        return (lax.cond(living, accumulate, unchanged, running), None)
    initial = (jnp.zeros((TIME, channels), jnp.float32), jnp.zeros((TIME,), jnp.float32))
    totals_end, unused = lax.scan(visit, initial, (starts, profile_index, living_mask))
    weighted, weight_total = totals_end
    return (weighted / jnp.maximum(weight_total, 1.0)[:, None]).astype(jnp.bfloat16)
```

```python
import functools
import math

import jax
import jax.numpy as jnp
from jax import lax
from jax.experimental import pallas as pl
from jax.experimental.pallas import tpu as pltpu
from jax.sharding import PartitionSpec as P

bf16, f32, i32 = jnp.bfloat16, jnp.float32, jnp.int32
MESH = pl.DeviceIdType.MESH
EPS = 1e-05
SEG = 256
HALO = 32
WSEG = 16
SHARD = 2048
NSEG = SHARD // SEG
SLOTS = 16
DEAD = -100000
G1 = math.sqrt(2.0 / math.pi)
G2 = G1 * 0.044715


def gelu32(v):
    half = 0.5 * v
    return half + half * jnp.tanh(v * (G1 + G2 * (v * v)))


def gelu16(v):
    v = v.astype(bf16)
    half = bf16(0.5) * v
    return half + half * jnp.tanh(v * (bf16(G1) + bf16(G2) * (v * v)))


def feature_kernel(
    count, table, stream, weight, bias, feats, norms, rows, stats, local_sem, halo_send, halo_recv,
    stat_send, stat_recv,
):
    me = lax.axis_index("tm")

    def at(offset):
        return lax.rem(me + offset + count, count)

    load = pltpu.make_async_copy(stream, rows.at[pl.ds(48, SHARD)], local_sem)
    load.start()
    barrier = pltpu.get_barrier_semaphore()
    for offset in (-2, -1, 1, 2):
        pl.semaphore_signal(barrier, inc=1, device_id=(at(offset),), device_id_type=MESH)
    pl.semaphore_wait(barrier, 4)
    to_right = pltpu.make_async_remote_copy(
        src_ref=stream.at[pl.ds(SHARD - 48, 48)], dst_ref=rows.at[pl.ds(0, 48)],
        send_sem=halo_send.at[0], recv_sem=halo_recv.at[0], device_id=(at(1),), device_id_type=MESH,
    )
    to_left = pltpu.make_async_remote_copy(
        src_ref=stream.at[pl.ds(0, 16)], dst_ref=rows.at[pl.ds(SHARD + 48, 16)],
        send_sem=halo_send.at[1], recv_sem=halo_recv.at[1], device_id=(at(-1),), device_id_type=MESH,
    )
    to_right.start()
    to_left.start()
    load.wait()

    def stem(first, length):
        block = rows[pl.ds(first + 32, length + 32)]
        wide = jnp.concatenate([block[13 + k : 13 + k + length] for k in range(7)], axis=1)
        summed = jnp.dot(wide, weight[...], preferred_element_type=f32) + bias[...]
        made = gelu32(summed).astype(bf16)
        feats[pl.ds(first + HALO, length)] = made
        return made.astype(f32)

    def tile(index):
        made = stem(index * 512, 512)
        for half in range(2):
            part = made[half * SEG : (half + 1) * SEG]
            row = 16 + index * 2 + half
            stats[0, row : row + 1] = jnp.sum(part, axis=0, keepdims=True)
            stats[1, row : row + 1] = jnp.sum(part * part, axis=0, keepdims=True)

    tile(1)
    tile(2)
    to_right.wait()
    to_left.wait()

    @pl.when(me == 0)
    def _():
        rows[pl.ds(0, 48)] = jnp.zeros((48, 128), bf16)

    @pl.when(me == count - 1)
    def _():
        rows[pl.ds(SHARD + 48, 16)] = jnp.zeros((16, 128), bf16)

    tile(3)
    tile(0)
    copies = []
    for index, offset in enumerate((-2, -1, 1, 2)):
        copies.append(
            pltpu.make_async_remote_copy(
                src_ref=stats.at[:, pl.ds(16, 8)], dst_ref=stats.at[:, pl.ds(8 * (2 - offset), 8)],
                send_sem=stat_send.at[index], recv_sem=stat_recv.at[index],
                device_id=(at(offset),), device_id_type=MESH,
            )
        )
    for copy in copies:
        copy.start()
    stem(-HALO, HALO)
    for copy in copies:
        copy.wait()
    for slot in range(SLOTS):
        owner = me + slot // 4 - 2
        inside = jnp.logical_and(owner >= 0, owner < count)
        start = jnp.where(inside, table[jnp.clip(owner, 0, count - 1) * 8 + slot % 4], 0)
        first = jnp.clip(start - NSEG * me + 16, 0, 24)
        row = lax.broadcasted_iota(i32, (40, 128), 0)
        covered = jnp.logical_and(row >= first, row < first + WSEG)
        mean, square = (
            jnp.sum(jnp.where(covered, stats[n], 0.0), axis=0, keepdims=True) * (1.0 / (WSEG * SEG))
            for n in range(2)
        )
        scale = lax.rsqrt(square - mean * mean + EPS)
        norms[slot : slot + 1] = scale
        norms[SLOTS + slot : SLOTS + slot + 1] = -mean * scale


def make_features(count, table, stream, weight, bias):
    return pl.pallas_call(
        functools.partial(feature_kernel, count),
        out_shape=[
            jax.ShapeDtypeStruct((SHARD + HALO, 128), bf16),
            jax.ShapeDtypeStruct((2 * SLOTS, 128), f32),
        ],
        in_specs=[
            pl.BlockSpec(memory_space=pltpu.SMEM),
            pl.BlockSpec(memory_space=pl.ANY),
            pl.BlockSpec(memory_space=pltpu.VMEM),
            pl.BlockSpec(memory_space=pltpu.VMEM),
        ],
        out_specs=[pl.BlockSpec(memory_space=pltpu.VMEM)] * 2,
        scratch_shapes=[
            pltpu.VMEM((SHARD + 64, 128), bf16),
            pltpu.VMEM((2, 40, 128), f32),
            pltpu.SemaphoreType.DMA,
            pltpu.SemaphoreType.DMA((2,)),
            pltpu.SemaphoreType.DMA((2,)),
            pltpu.SemaphoreType.DMA((4,)),
            pltpu.SemaphoreType.DMA((4,)),
        ],
        compiler_params=pltpu.CompilerParams(
            collective_id=0, has_side_effects=True, vmem_limit_bytes=24 * 2**20
        ),
    )(table, stream, weight, bias)


BIG, SMALL = 2048, 512
CAPACITY = 128 * SEG + 64 * HALO + BIG
UNITS = 160


def network_kernel(
    count, table, feats, norms, first_weight, deep_weight, layer_bias, head_weight, head_bias,
    profiles, out, x_stack, h_a, h_b, total, columns, padded, weights, unit, zeros,
):
    me = lax.axis_index("tm")

    padded[...] = jnp.zeros_like(padded)
    for p in range(4):
        for k in range(WSEG):
            padded[p * 32 + 8 + k : p * 32 + 9 + k] = profiles[p : p + 1, k * SEG : (k + 1) * SEG]
    for block in range(32):
        part = profiles[:, block * 128 : (block + 1) * 128]
        part = jnp.concatenate([part, jnp.zeros((4, 128), f32)], axis=0)
        columns[block * 128 : (block + 1) * 128] = part.T
    weights[...] = jnp.zeros_like(weights)

    def clear(index, carry):
        total[pl.ds(pl.multiple_of(index * SEG, SEG), SEG)] = jnp.zeros((SEG, 128), f32)
        return carry

    lax.fori_loop(0, NSEG, clear, 0)

    def own_slot(slot, state):
        owner = me + slot // 4 - 2
        inside = jnp.logical_and(owner >= 0, owner < count)
        place = jnp.clip(owner, 0, count - 1) * 8 + lax.rem(slot, 4)
        start = jnp.where(inside, table[place], DEAD)
        profile = table[place + 4]
        rel = start - NSEG * me
        low, high = jnp.maximum(rel, 0), jnp.minimum(rel + WSEG, NSEG)
        scale = norms[pl.ds(slot, 1)]
        shift = norms[pl.ds(SLOTS + slot, 1)]

        def normalised(row, length):
            block = feats[pl.ds(pl.multiple_of(row, 32), length)].astype(f32)
            return (block * scale + shift).astype(bf16)

        def begin(state):
            rows, units, blanks = state
            rows = pl.multiple_of(rows, 32)
            for k in range(NSEG):
                weights[k : k + 1] += padded[pl.ds(profile * 32 + 8 - rel + k, 1)]

            @pl.when(rel >= 0)
            def _():
                x_stack[pl.ds(rows + HALO, HALO)] = jnp.zeros((HALO, 128), bf16)
                zeros[blanks] = rows + HALO

            @pl.when(rel < 0)
            def _():
                x_stack[pl.ds(rows + HALO, HALO)] = normalised(low * SEG, HALO)

            return rows + HALO, units, blanks + jnp.where(rel >= 0, 1, 0)

        def segment(k, state):
            rows, units, blanks = state
            rows = pl.multiple_of(rows, 32)
            x_stack[pl.ds(rows + HALO, SEG)] = normalised(k * SEG + HALO, SEG)
            unit[0, units] = rows
            unit[1, units] = k
            unit[2, units] = (k - rel) * SEG
            unit[3, units] = profile
            return rows + SEG, units + 1, blanks

        state = lax.cond(high > low, begin, lambda s: s, state)
        return lax.fori_loop(low, high, segment, state)

    rows, units, blanks = lax.fori_loop(0, SLOTS, own_slot, (i32(0), i32(0), i32(0)))

    big = rows // BIG
    left = rows - big * BIG
    small = (left + SMALL - 1) // SMALL

    def over_rows(body):
        def big_step(index, carry):
            body(pl.multiple_of(index * BIG, BIG), BIG)
            return carry

        def small_step(index, carry):
            body(pl.multiple_of(big * BIG + index * SMALL, SMALL), SMALL)
            return carry

        lax.fori_loop(0, big, big_step, 0)
        lax.fori_loop(0, small, small_step, 0)

    def layer(index, source, target, weight):
        spread = 2**index

        def body(first, length):
            block = source[pl.ds(first, length + HALO)]
            wide = jnp.concatenate(
                [block[HALO - s * spread : HALO - s * spread + length] for s in (2, 1, 0)], axis=1
            )
            summed = jnp.dot(wide, weight, preferred_element_type=f32)
            made = gelu16(summed + layer_bias[index : index + 1])
            if index:
                made = made + block[HALO:]
            target[pl.ds(first + HALO, length)] = made

        over_rows(body)

        def blank(n, carry):
            target[pl.ds(pl.multiple_of(zeros[n], 32), HALO)] = jnp.zeros((HALO, 256), bf16)
            return carry

        lax.fori_loop(0, blanks, blank, 0)

    layer(0, x_stack, h_a, first_weight[...])
    layer(1, h_a, h_b, deep_weight[0])
    layer(2, h_b, h_a, deep_weight[1])
    layer(3, h_a, h_b, deep_weight[2])

    def head(first, length):
        made = jnp.dot(
            h_b[pl.ds(first + HALO, length)], head_weight[...], preferred_element_type=f32
        )
        x_stack[pl.ds(first + HALO, length)] = (made + head_bias[...]).astype(bf16)

    over_rows(head)

    def gather(n, carry):
        rows = pl.multiple_of(unit[0, n] + HALO, 32)
        target = pl.ds(pl.multiple_of(unit[1, n] * SEG, SEG), SEG)
        offset = pl.ds(pl.multiple_of(unit[2, n], SEG), SEG)
        for p in range(4):

            @pl.when(unit[3, n] == p)
            def _():
                made = x_stack[pl.ds(rows, SEG)].astype(f32)
                total[target] += made * columns[offset, p : p + 1]

        return carry

    lax.fori_loop(0, units, gather, 0)

    inverse = 1.0 / jnp.maximum(weights[...], 1.0)
    for half in range(2):
        column = inverse[:, half * 128 : (half + 1) * 128].T
        for k in range(NSEG):
            where = pl.ds(k * SEG + half * 128, 128)
            out[where] = (total[where] * column[:, k : k + 1]).astype(bf16)


def run_network(count, table, feats, norms, net, profiles):
    vmem = pl.BlockSpec(memory_space=pltpu.VMEM)
    return pl.pallas_call(
        functools.partial(network_kernel, count),
        out_shape=jax.ShapeDtypeStruct((SHARD, 128), bf16),
        in_specs=[pl.BlockSpec(memory_space=pltpu.SMEM)] + [vmem] * 8,
        out_specs=vmem,
        scratch_shapes=[
            pltpu.VMEM((CAPACITY + HALO, 128), bf16),
            pltpu.VMEM((CAPACITY + HALO, 256), bf16),
            pltpu.VMEM((CAPACITY + HALO, 256), bf16),
            pltpu.VMEM((SHARD, 128), f32),
            pltpu.VMEM((4096, 8), f32),
            pltpu.VMEM((4 * 32, SEG), f32),
            pltpu.VMEM((NSEG, SEG), f32),
            pltpu.SMEM((4, UNITS), i32),
            pltpu.SMEM((UNITS,), i32),
        ],
        compiler_params=pltpu.CompilerParams(vmem_limit_bytes=60 * 2**20),
    )(table, feats, norms, *net, profiles)


def per_device(
    stream, stem_weight, stem_bias, first_weight, deep_weight, layer_bias, head_weight, head_bias,
    profiles, starts, profile_index, counts,
):
    count = lax.axis_size("tm")
    live = jnp.arange(4, dtype=i32) < counts[0]
    mine = jnp.concatenate([jnp.where(live, starts // SEG, DEAD), profile_index])
    table = lax.all_gather(mine, "tm", tiled=True)
    feats, norms = make_features(
        count, table, stream, stem_weight.reshape(7 * 128, 128), stem_bias.reshape(1, 128)
    )
    net = (
        first_weight.reshape(3 * 128, 256),
        deep_weight.reshape(3, 3 * 256, 256),
        layer_bias,
        head_weight,
        head_bias.reshape(1, 128),
    )
    return run_network(count, table, feats, norms, net, profiles)


def solution(mesh):
    in_specs = (P("tm", None), P(), P(), P(), P(), P(), P(), P(), P(), P("tm"), P("tm"), P("tm"))
    return jax.shard_map(
        per_device, mesh=mesh, in_specs=in_specs, out_specs=P("tm", None), check_vma=False
    )
```

```python
import functools
import math

import jax
import jax.numpy as jnp
from jax import lax
from jax.experimental import pallas as pl
from jax.experimental.pallas import tpu as pltpu
from jax.sharding import PartitionSpec as P

bf16, f32, i32 = jnp.bfloat16, jnp.float32, jnp.int32
MESH = pl.DeviceIdType.MESH
EPS = 1e-05
SEG = 256
HALO = 32
WSEG = 16
SHARD = 2048
NSEG = SHARD // SEG
SLOTS = 16
DEAD = -100000
G1 = math.sqrt(2.0 / math.pi)
G2 = G1 * 0.044715


def gelu32(v):
    half = 0.5 * v
    return half + half * jnp.tanh(v * (G1 + G2 * (v * v)))


def gelu16(v):
    v = v.astype(bf16)
    half = bf16(0.5) * v
    return half + half * jnp.tanh(v * (bf16(G1) + bf16(G2) * (v * v)))


def other_core(d):
    return d + 1 - 2 * (d % 2)


def along_y(d, step):
    return (d + 32 * step + 128) % 128


def along_z(d, step):
    return d // 32 * 32 + (d % 32 + 8 * step + 32) % 32


def along_x(d, step):
    return d // 8 * 8 + (d % 8 + 2 * step + 8) % 8


def helper(d, k):
    if k == 0:
        return other_core(along_y(d, 1))
    if k == 1:
        return along_y(d, -1)
    if k == 2:
        return other_core(along_z(d, 1))
    return along_z(d, -1)


def helped(d, k):
    if k == 0:
        return along_y(other_core(d), -1)
    if k == 1:
        return along_y(d, 1)
    if k == 2:
        return along_z(other_core(d), -1)
    return along_z(d, 1)


def lanes_core(v, lane):
    return jnp.where(lane % 2 == 0, pltpu.roll(v, 127, 1), pltpu.roll(v, 1, 1))


def lanes_y(v, lane, step):
    return pltpu.roll(v, 96 if step > 0 else 32, 1)


def lanes_z(v, lane, step):
    if step > 0:
        return jnp.where(lane % 32 < 24, pltpu.roll(v, 120, 1), pltpu.roll(v, 24, 1))
    return jnp.where(lane % 32 >= 8, pltpu.roll(v, 8, 1), pltpu.roll(v, 104, 1))


def at_helper(v, lane, k):
    if k == 0:
        return lanes_y(lanes_core(v, lane), lane, 1)
    if k == 1:
        return lanes_y(v, lane, -1)
    if k == 2:
        return lanes_z(lanes_core(v, lane), lane, 1)
    return lanes_z(v, lane, -1)


def at_helped(v, lane, k):
    if k == 0:
        return lanes_core(lanes_y(v, lane, -1), lane)
    if k == 1:
        return lanes_y(v, lane, 1)
    if k == 2:
        return lanes_core(lanes_z(v, lane, -1), lane)
    return lanes_z(v, lane, 1)


def share_out(rows):
    lane = lax.broadcasted_iota(i32, (8, 128), 1)
    segment = (lane * NSEG + lax.broadcasted_iota(i32, (8, 128), 0)).astype(f32)
    covering = jnp.zeros((8, 128), f32)
    for j in range(4):
        start = jnp.broadcast_to(rows[j : j + 1], (8, 128))
        for offset in range(-2, 2):
            moved = pltpu.roll(start, (-offset) % 128, 1) if offset else start
            there = jnp.logical_and(lane + offset >= 0, lane + offset < 128)
            there = jnp.logical_and(there, jnp.logical_and(segment >= moved, segment < moved + WSEG))
            covering = covering + jnp.where(there, 1.0, 0.0)
    caps = [
        jnp.broadcast_to(covering[2 * k : 2 * k + 1] + covering[2 * k + 1 : 2 * k + 2], (8, 128))
        for k in range(4)
    ]
    load = caps[0] + caps[1] + caps[2] + caps[3]
    given = [jnp.zeros((8, 128), f32) for _ in range(4)]
    for _ in range(4):
        for k in range(4):
            half = 0.5 * (load - at_helper(load, lane, k))
            move = jnp.where(half >= 0, jnp.floor(half), -jnp.floor(-half))
            move = jnp.clip(move, -given[k], caps[k] - given[k])
            given[k] = given[k] + move
            load = load - move + at_helped(move, lane, k)
    return given


def feature_kernel(
    count, starts, profile_index, live, stream, weight_hbm, bias, feats, norms, table, shares, lent, lent_norms,
    rows, weight, stats, known, local_sem, halo_send, halo_recv, stat_send, stat_recv, known_send, known_recv,
    lent_send, lent_recv, norm_send, norm_recv,
):
    me = lax.axis_index("tm")

    def at(offset):
        return lax.rem(me + offset + count, count)

    load = pltpu.make_async_copy(stream, rows.at[pl.ds(48, SHARD)], local_sem.at[0])
    load.start()
    load_weight = pltpu.make_async_copy(weight_hbm, weight, local_sem.at[1])
    load_weight.start()

    lane = lax.broadcasted_iota(i32, (1, 128), 1)
    line = jnp.zeros((1, 128), f32)
    for j in range(4):
        start = jnp.where(j < live[0], starts[j] // SEG, DEAD).astype(f32)
        line = jnp.where(lane == j, start, line)
        line = jnp.where(lane == 4 + j, profile_index[j].astype(f32), line)
    known[me] = line

    barrier = pltpu.get_barrier_semaphore()
    partners = [at(offset) for offset in (-2, -1, 1, 2)] + [other_core(me)]
    for step in (1, 2, 3):
        partners += [along_x(me, step), along_y(me, step), along_z(me, step)]
    for k in range(4):
        partners += [helper(me, k), helped(me, k)]
    for partner in partners:
        pl.semaphore_signal(barrier, inc=1, device_id=(partner,), device_id_type=MESH)
    pl.semaphore_wait(barrier, len(partners))

    def send(src, dst, send_sem, recv_sem, device):
        copy = pltpu.make_async_remote_copy(
            src_ref=src, dst_ref=dst, send_sem=send_sem, recv_sem=recv_sem, device_id=(device,),
            device_id_type=MESH,
        )
        copy.start()
        return copy

    def tell(first, length, index, device):
        block = known.at[pl.ds(first, length)]
        return send(block, block, known_send.at[index], known_recv.at[index], device)

    halos = [
        send(stream.at[pl.ds(SHARD - 48, 48)], rows.at[pl.ds(0, 48)], halo_send.at[0], halo_recv.at[0], at(1)),
        send(stream.at[pl.ds(0, 16)], rows.at[pl.ds(SHARD + 48, 16)], halo_send.at[1], halo_recv.at[1], at(-1)),
    ]
    round_c = tell(me, 1, 0, other_core(me))
    load.wait()
    load_weight.wait()

    def stem(first, length):
        block = rows[pl.ds(first + 32, length + 32)]
        wide = jnp.concatenate([block[13 + k : 13 + k + length] for k in range(7)], axis=1)
        summed = jnp.dot(wide, weight[...], preferred_element_type=f32) + bias[...]
        made = gelu32(summed).astype(bf16)
        feats[pl.ds(first + HALO, length)] = made
        return made.astype(f32)

    def tile(index):
        made = stem(index * 512, 512)
        for half in range(2):
            part = made[half * SEG : (half + 1) * SEG]
            row = 16 + index * 2 + half
            stats[0, row : row + 1] = jnp.sum(part, axis=0, keepdims=True)
            stats[1, row : row + 1] = jnp.sum(part * part, axis=0, keepdims=True)

    def lend(k):
        return send(
            feats.at[pl.ds(512 * k, 512 + HALO)], lent.at[k], lent_send.at[k], lent_recv.at[k], helper(me, k)
        )

    tile(1)
    round_c.wait()
    round_x = [tell(me // 2 * 2, 2, step, along_x(me, step)) for step in (1, 2, 3)]
    tile(2)
    loans = [lend(2)]
    for copy in round_x:
        copy.wait()
    round_z = [tell(me // 8 * 8, 8, 3 + step, along_z(me, step)) for step in (1, 2, 3)]
    for copy in halos:
        copy.wait()

    @pl.when(me == 0)
    def _():
        rows[pl.ds(0, 48)] = jnp.zeros((48, 128), bf16)

    @pl.when(me == count - 1)
    def _():
        rows[pl.ds(SHARD + 48, 16)] = jnp.zeros((16, 128), bf16)

    tile(3)
    loans.append(lend(3))
    for copy in round_z:
        copy.wait()
    round_y = [tell(me // 32 * 32, 32, 6 + step, along_y(me, step)) for step in (1, 2, 3)]
    tile(0)
    moments = [
        send(
            stats.at[:, pl.ds(16, 8)], stats.at[:, pl.ds(8 * (2 - offset), 8)], stat_send.at[index],
            stat_recv.at[index], at(offset),
        )
        for index, offset in enumerate((-2, -1, 1, 2))
    ]
    loans.append(lend(1))
    stem(-HALO, HALO)
    loans.append(lend(0))
    for copy in round_y:
        copy.wait()
    for copy in moments:
        copy.wait()

    row = lax.broadcasted_iota(i32, (40, 128), 0).astype(f32)
    for slot in range(SLOTS):
        owner = jnp.clip(me + slot // 4 - 2, 0, count - 1)
        start = known[owner][:, slot % 4 : slot % 4 + 1]
        first = start - (NSEG * me - 16).astype(f32)
        covered = jnp.logical_and(row >= first, row < first + WSEG)
        mean, square = (
            jnp.sum(jnp.where(covered, stats[n], 0.0), axis=0, keepdims=True) * (1.0 / (WSEG * SEG))
            for n in range(2)
        )
        scale = lax.rsqrt(square - mean * mean + EPS)
        norms[slot : slot + 1] = scale
        norms[SLOTS + slot : SLOTS + slot + 1] = -mean * scale
    for k in range(4):
        loans.append(send(norms, lent_norms.at[k], norm_send.at[k], norm_recv.at[k], helper(me, k)))

    turned = known[...].reshape(128, 128).T[:8]
    table[...] = turned.astype(i32)
    given = share_out(turned)
    shares[...] = jnp.concatenate([given[k][:1] for k in range(4)] + [jnp.zeros((4, 128), f32)], axis=0).astype(i32)
    for copy in loans:
        copy.wait()


def make_features(count, starts, profile_index, counts, stream, weight, bias):
    vmem, smem, hbm = (pl.BlockSpec(memory_space=m) for m in (pltpu.VMEM, pltpu.SMEM, pl.ANY))
    dma = pltpu.SemaphoreType.DMA
    return pl.pallas_call(
        functools.partial(feature_kernel, count),
        out_shape=[
            jax.ShapeDtypeStruct((SHARD + HALO, 128), bf16),
            jax.ShapeDtypeStruct((2 * SLOTS, 128), f32),
            jax.ShapeDtypeStruct((8, 128), i32),
            jax.ShapeDtypeStruct((8, 128), i32),
            jax.ShapeDtypeStruct((4, 512 + HALO, 128), bf16),
            jax.ShapeDtypeStruct((4, 2 * SLOTS, 128), f32),
        ],
        in_specs=[smem, smem, smem, hbm, hbm, vmem],
        out_specs=[vmem, vmem, vmem, vmem, hbm, hbm],
        scratch_shapes=[
            pltpu.VMEM((SHARD + 64, 128), bf16),
            pltpu.VMEM((7 * 128, 128), bf16),
            pltpu.VMEM((2, 40, 128), f32),
            pltpu.VMEM((128, 1, 128), f32),
            dma((2,)),
            dma((2,)), dma((2,)),
            dma((4,)), dma((4,)),
            dma((10,)), dma((10,)),
            dma((4,)), dma((4,)),
            dma((4,)), dma((4,)),
        ],
        compiler_params=pltpu.CompilerParams(
            collective_id=0, has_side_effects=True, vmem_limit_bytes=56 * 2**20
        ),
    )(starts, profile_index, counts, stream, weight, bias)


BIG, SMALL = 2048, 512
CAPACITY = 128 * SEG + 128 * HALO + BIG
UNITS = 160


def network_kernel(
    count, table, shares, feats_hbm, lent_hbm, norms_hbm, lent_norms_hbm, first_hbm, deep_hbm, layer_bias, head_hbm,
    head_bias, profiles, sums, weights, lent_sums, feats, norms, first_weight, deep_weight, head_weight, x_stack, h_a,
    h_b, total, columns, padded, unit, zeros, sems,
):
    me = lax.axis_index("tm")
    pieces = [
        (feats_hbm, feats.at[pl.ds(0, SHARD + HALO)]),
        (norms_hbm, norms.at[pl.ds(0, 2 * SLOTS)]),
        (first_hbm, first_weight),
        (deep_hbm, deep_weight),
        (head_hbm, head_weight),
    ]
    for k in range(4):
        pieces.append((lent_hbm.at[k], feats.at[pl.ds(SHARD + HALO + (512 + HALO) * k, 512 + HALO)]))
        pieces.append((lent_norms_hbm.at[k], norms.at[pl.ds(2 * SLOTS * (k + 1), 2 * SLOTS)]))
    loads = [pltpu.make_async_copy(src, dst, sems.at[n]) for n, (src, dst) in enumerate(pieces)]
    for copy in loads:
        copy.start()

    padded[...] = jnp.zeros_like(padded)
    for p in range(4):
        for k in range(WSEG):
            padded[p * 32 + 8 + k : p * 32 + 9 + k] = profiles[p : p + 1, k * SEG : (k + 1) * SEG]
    for block in range(32):
        part = profiles[:, block * 128 : (block + 1) * 128]
        part = jnp.concatenate([part, jnp.zeros((4, 128), f32)], axis=0)
        columns[block * 128 : (block + 1) * 128] = part.T
    weights[...] = jnp.zeros_like(weights)

    def clear(index, carry):
        total[pl.ds(pl.multiple_of(index * SEG, SEG), SEG)] = jnp.zeros((SEG, 128), f32)
        return carry

    lax.fori_loop(0, 2 * NSEG, clear, 0)
    for copy in loads:
        copy.wait()

    def window(home, slot):
        owner = home + slot // 4 - 2
        inside = jnp.logical_and(owner >= 0, owner < count)
        owner = jnp.clip(owner, 0, count - 1)
        start = jnp.where(inside, table[lax.rem(slot, 4), owner], DEAD)
        return start - NSEG * home, table[4 + lax.rem(slot, 4), owner]

    def put(base, target, norm, slot, rel, profile, low, high, fresh, state):
        scale = norms[pl.ds(norm + slot, 1)]
        shift = norms[pl.ds(norm + SLOTS + slot, 1)]

        def normalised(row, length):
            block = feats[pl.ds(pl.multiple_of(row, 32), length)].astype(f32)
            return (block * scale + shift).astype(bf16)

        def begin(state):
            rows, units, blanks = state
            rows = pl.multiple_of(rows, 32)

            @pl.when(low == rel)
            def _():
                x_stack[pl.ds(rows + HALO, HALO)] = jnp.zeros((HALO, 128), bf16)
                zeros[blanks] = rows + HALO

            @pl.when(low != rel)
            def _():
                x_stack[pl.ds(rows + HALO, HALO)] = normalised(base + low * SEG, HALO)

            return rows + HALO, units, blanks + jnp.where(low == rel, 1, 0)

        def segment(k, state):
            rows, units, blanks = state
            rows = pl.multiple_of(rows, 32)
            x_stack[pl.ds(rows + HALO, SEG)] = normalised(base + k * SEG + HALO, SEG)
            unit[0, units] = rows
            unit[1, units] = target + k * SEG
            unit[2, units] = (k - rel) * SEG
            unit[3, units] = profile
            return rows + SEG, units + 1, blanks

        state = lax.cond(fresh, begin, lambda s: s, state)
        return lax.fori_loop(low, high, segment, state)

    def own_slot(slot, carry):
        rel, profile = window(me, slot)

        def covered(carry):
            for k in range(NSEG):
                weights[k : k + 1] += padded[pl.ds(profile * 32 + 8 - rel + k, 1)]
            state, lefts = carry[:3], list(carry[3:])
            end = i32(-1)
            for k in range(4):
                first = jnp.maximum(rel, 2 * k)
                high = jnp.minimum(rel + WSEG, 2 * k + 2)
                given = jnp.minimum(lefts[k], jnp.maximum(high - first, 0))
                lefts[k] = lefts[k] - given
                low = first + given
                fresh = jnp.logical_and(high > low, low != end)
                state = put(0, 0, 0, slot, rel, profile, low, high, fresh, state)
                end = jnp.where(high > low, high, end)
            return (*state, *lefts)

        return lax.cond(jnp.logical_and(rel > -WSEG, rel < NSEG), covered, lambda c: c, carry)

    carry = lax.fori_loop(0, SLOTS, own_slot, (i32(0), i32(0), i32(0), *(shares[k, me] for k in range(4))))
    state = carry[:3]
    for k in range(4):
        home = helped(me, k)
        share = shares[k, home]

        def lent_slot(slot, carry, k=k, home=home):
            rel, profile = window(home, slot)
            first = jnp.maximum(rel, 2 * k)
            taken = jnp.minimum(carry[3], jnp.maximum(jnp.minimum(rel + WSEG, 2 * k + 2) - first, 0))
            state = put(
                SHARD + HALO + HALO * k, SHARD, 2 * SLOTS * (k + 1), slot, rel, profile, first, first + taken,
                taken > 0, carry[:3],
            )
            return (*state, carry[3] - taken)

        state = lax.fori_loop(0, jnp.where(share > 0, SLOTS, 0), lent_slot, (*state, share))[:3]
    rows, units, blanks = state

    big = rows // BIG
    left = rows - big * BIG
    small = (left + SMALL - 1) // SMALL

    def over_rows(body):
        def big_step(index, carry):
            body(pl.multiple_of(index * BIG, BIG), BIG)
            return carry

        def small_step(index, carry):
            body(pl.multiple_of(big * BIG + index * SMALL, SMALL), SMALL)
            return carry

        lax.fori_loop(0, big, big_step, 0)
        lax.fori_loop(0, small, small_step, 0)

    def layer(index, source, target, weight):
        spread = 2**index

        def body(first, length):
            block = source[pl.ds(first, length + HALO)]
            wide = jnp.concatenate(
                [block[HALO - s * spread : HALO - s * spread + length] for s in (2, 1, 0)], axis=1
            )
            summed = jnp.dot(wide, weight, preferred_element_type=f32)
            made = gelu16(summed + layer_bias[index : index + 1])
            if index:
                made = made + block[HALO:]
            target[pl.ds(first + HALO, length)] = made

        over_rows(body)

        def blank(n, carry):
            target[pl.ds(pl.multiple_of(zeros[n], 32), HALO)] = jnp.zeros((HALO, 256), bf16)
            return carry

        lax.fori_loop(0, blanks, blank, 0)

    layer(0, x_stack, h_a, first_weight[...])
    layer(1, h_a, h_b, deep_weight[0])
    layer(2, h_b, h_a, deep_weight[1])
    layer(3, h_a, h_b, deep_weight[2])

    def head(first, length):
        made = jnp.dot(
            h_b[pl.ds(first + HALO, length)], head_weight[...], preferred_element_type=f32
        )
        x_stack[pl.ds(first + HALO, length)] = (made + head_bias[...]).astype(bf16)

    over_rows(head)

    def gather(n, carry):
        rows = pl.multiple_of(unit[0, n] + HALO, 32)
        target = pl.ds(pl.multiple_of(unit[1, n], SEG), SEG)
        offset = pl.ds(pl.multiple_of(unit[2, n], SEG), SEG)
        for p in range(4):

            @pl.when(unit[3, n] == p)
            def _():
                made = x_stack[pl.ds(rows, SEG)].astype(f32)
                total[target] += made * columns[offset, p : p + 1]

        return carry

    lax.fori_loop(0, units, gather, 0)

    def store(index, carry):
        where = pl.ds(pl.multiple_of(index * 512, 512), 512)
        sums[where] = total[where].astype(bf16)
        lent_sums[index] = total[pl.ds(pl.multiple_of(SHARD + index * 512, 512), 512)].astype(bf16)
        return carry

    lax.fori_loop(0, 4, store, 0)


def run_network(count, table, shares, feats, lent, norms, lent_norms, net, profiles):
    vmem, smem, hbm = (pl.BlockSpec(memory_space=m) for m in (pltpu.VMEM, pltpu.SMEM, pl.ANY))
    first_weight, deep_weight, layer_bias, head_weight, head_bias = net
    return pl.pallas_call(
        functools.partial(network_kernel, count),
        out_shape=[
            jax.ShapeDtypeStruct((SHARD, 128), bf16),
            jax.ShapeDtypeStruct((NSEG, SEG), f32),
            jax.ShapeDtypeStruct((4, 512, 128), bf16),
        ],
        in_specs=[smem, smem, hbm, hbm, hbm, hbm, hbm, hbm, vmem, hbm, vmem, vmem],
        out_specs=[vmem, vmem, vmem],
        scratch_shapes=[
            pltpu.VMEM((SHARD + HALO + 4 * (512 + HALO), 128), bf16),
            pltpu.VMEM((10 * SLOTS, 128), f32),
            pltpu.VMEM((384, 256), bf16),
            pltpu.VMEM((3, 768, 256), bf16),
            pltpu.VMEM((256, 128), bf16),
            pltpu.VMEM((CAPACITY + HALO, 128), bf16),
            pltpu.VMEM((CAPACITY + HALO, 256), bf16),
            pltpu.VMEM((CAPACITY + HALO, 256), bf16),
            pltpu.VMEM((2 * SHARD, 128), f32),
            pltpu.VMEM((4096, 8), f32),
            pltpu.VMEM((4 * 32, SEG), f32),
            pltpu.SMEM((4, UNITS), i32),
            pltpu.SMEM((UNITS,), i32),
            pltpu.SemaphoreType.DMA((13,)),
        ],
        compiler_params=pltpu.CompilerParams(vmem_limit_bytes=62 * 2**20),
    )(table, shares, feats, lent, norms, lent_norms, first_weight, deep_weight, layer_bias, head_weight, head_bias, profiles)


def return_kernel(lent_sums, sums, weights, out, arrived, send_sem, recv_sem):
    me = lax.axis_index("tm")
    barrier = pltpu.get_barrier_semaphore()
    for k in range(4):
        for partner in (helper(me, k), helped(me, k)):
            pl.semaphore_signal(barrier, inc=1, device_id=(partner,), device_id_type=MESH)
    pl.semaphore_wait(barrier, 8)
    copies = []
    for k in range(4):
        copy = pltpu.make_async_remote_copy(
            src_ref=lent_sums.at[k], dst_ref=arrived.at[k], send_sem=send_sem.at[k], recv_sem=recv_sem.at[k],
            device_id=(helped(me, k),), device_id_type=MESH,
        )
        copy.start()
        copies.append(copy)
    inverse = 1.0 / jnp.maximum(weights[...], 1.0)
    columns = [inverse[:, half * 128 : (half + 1) * 128].T for half in range(2)]
    for k in range(4):
        copies[k].wait()
        for part in range(4):
            row = part * 128
            column = columns[part % 2][:, 2 * k + part // 2 : 2 * k + part // 2 + 1]
            made = sums[pl.ds(512 * k + row, 128)].astype(f32) + arrived[k, pl.ds(row, 128)].astype(f32)
            out[pl.ds(512 * k + row, 128)] = (made * column).astype(bf16)


def bring_back(lent_sums, sums, weights):
    vmem = pl.BlockSpec(memory_space=pltpu.VMEM)
    return pl.pallas_call(
        return_kernel,
        out_shape=jax.ShapeDtypeStruct((SHARD, 128), bf16),
        in_specs=[pl.BlockSpec(memory_space=pl.ANY), vmem, vmem],
        out_specs=vmem,
        scratch_shapes=[
            pltpu.VMEM((4, 512, 128), bf16),
            pltpu.SemaphoreType.DMA((4,)),
            pltpu.SemaphoreType.DMA((4,)),
        ],
        compiler_params=pltpu.CompilerParams(
            collective_id=1, has_side_effects=True, vmem_limit_bytes=56 * 2**20
        ),
    )(lent_sums, sums, weights)


def per_device(
    stream, stem_weight, stem_bias, first_weight, deep_weight, layer_bias, head_weight, head_bias,
    profiles, starts, profile_index, counts,
):
    count = lax.axis_size("tm")
    feats, norms, table, shares, lent, lent_norms = make_features(
        count, starts, profile_index, counts, stream, stem_weight.reshape(7 * 128, 128), stem_bias.reshape(1, 128)
    )
    net = (
        first_weight.reshape(3 * 128, 256),
        deep_weight.reshape(3, 3 * 256, 256),
        layer_bias,
        head_weight,
        head_bias.reshape(1, 128),
    )
    sums, weights, lent_sums = run_network(count, table, shares, feats, lent, norms, lent_norms, net, profiles)
    return bring_back(lent_sums, sums, weights)


def solution(mesh):
    in_specs = (P("tm", None), P(), P(), P(), P(), P(), P(), P(), P(), P("tm"), P("tm"), P("tm"))
    return jax.shard_map(
        per_device, mesh=mesh, in_specs=in_specs, out_specs=P("tm", None), check_vma=False
    )
```

```python
import functools
import math

import jax
import jax.numpy as jnp
from jax import lax
from jax.experimental import pallas as pl
from jax.experimental.pallas import tpu as pltpu
from jax.sharding import PartitionSpec as P

bf16, f32, i32 = jnp.bfloat16, jnp.float32, jnp.int32
MESH = pl.DeviceIdType.MESH
EPS = 1e-05
SEG = 256
HALO = 32
WSEG = 16
SHARD = 2048
NSEG = SHARD // SEG
SLOTS = 16
TAIL = 48
EDGE = TAIL + HALO
DEAD = -100000
G1 = math.sqrt(2.0 / math.pi)
G2 = G1 * 0.044715


def gelu32(v):
    half = 0.5 * v
    return half + half * jnp.tanh(v * (G1 + G2 * (v * v)))


def gelu16(v):
    v = v.astype(bf16)
    half = bf16(0.5) * v
    return half + half * jnp.tanh(v * (bf16(G1) + bf16(G2) * (v * v)))


def coordinates(d):
    return lax.div(d, 32), lax.rem(lax.div(d, 8), 4), lax.rem(lax.div(d, 2), 4), lax.rem(d, 2)


def device_at(y, z, x, core):
    return y * 32 + z * 8 + x * 2 + core


def helper(place, k):
    y, z, x, core = place
    if k == 0:
        return device_at(lax.rem(y + 1, 4), z, x, 1 - core)
    if k == 1:
        return device_at(lax.rem(y + 3, 4), z, x, core)
    if k == 2:
        return device_at(y, lax.rem(z + 1, 4), x, 1 - core)
    return device_at(y, lax.rem(z + 3, 4), x, core)


def helped(place, k):
    y, z, x, core = place
    if k == 0:
        return device_at(lax.rem(y + 3, 4), z, x, 1 - core)
    if k == 1:
        return device_at(lax.rem(y + 1, 4), z, x, core)
    if k == 2:
        return device_at(y, lax.rem(z + 3, 4), x, 1 - core)
    return device_at(y, lax.rem(z + 1, 4), x, core)


def lanes_core(v, lane):
    return jnp.where(lane % 2 == 0, pltpu.roll(v, 127, 1), pltpu.roll(v, 1, 1))


def lanes_y(v, lane, step):
    return pltpu.roll(v, 96 if step > 0 else 32, 1)


def lanes_z(v, lane, step):
    if step > 0:
        return jnp.where(lane % 32 < 24, pltpu.roll(v, 120, 1), pltpu.roll(v, 24, 1))
    return jnp.where(lane % 32 >= 8, pltpu.roll(v, 8, 1), pltpu.roll(v, 104, 1))


def at_helper(v, lane, k):
    if k == 0:
        return lanes_y(lanes_core(v, lane), lane, 1)
    if k == 1:
        return lanes_y(v, lane, -1)
    if k == 2:
        return lanes_z(lanes_core(v, lane), lane, 1)
    return lanes_z(v, lane, -1)


def at_helped(v, lane, k):
    if k == 0:
        return lanes_core(lanes_y(v, lane, -1), lane)
    if k == 1:
        return lanes_y(v, lane, 1)
    if k == 2:
        return lanes_core(lanes_z(v, lane, -1), lane)
    return lanes_z(v, lane, 1)


def share_out(rows):
    lane = lax.broadcasted_iota(i32, (8, 128), 1)
    segment = (lane * NSEG + lax.broadcasted_iota(i32, (8, 128), 0)).astype(f32)
    covering = jnp.zeros((8, 128), f32)
    for j in range(4):
        start = jnp.broadcast_to(rows[j : j + 1], (8, 128))
        for offset in range(-2, 2):
            moved = pltpu.roll(start, (-offset) % 128, 1) if offset else start
            there = jnp.logical_and(lane + offset >= 0, lane + offset < 128)
            there = jnp.logical_and(there, jnp.logical_and(segment >= moved, segment < moved + WSEG))
            covering = covering + jnp.where(there, 1.0, 0.0)
    caps = [
        jnp.broadcast_to(covering[2 * k : 2 * k + 1] + covering[2 * k + 1 : 2 * k + 2], (8, 128))
        for k in range(4)
    ]
    load = caps[0] + caps[1] + caps[2] + caps[3]
    given = [jnp.zeros((8, 128), f32) for _ in range(4)]
    for _ in range(4):
        for k in range(4):
            half = 0.5 * (load - at_helper(load, lane, k))
            move = jnp.where(half >= 0, jnp.floor(half), -jnp.floor(-half))
            move = jnp.clip(move, -given[k], caps[k] - given[k])
            given[k] = given[k] + move
            load = load - move + at_helped(move, lane, k)
    return given


def feature_kernel(
    count, starts, profile_index, live, stream, weight_hbm, bias, feats, norms, table, shares, lent, lent_norms,
    rows, weight, stats, mine, known, nearby, edge, local_sem, edge_send, edge_recv, line_send, line_recv, stat_send,
    stat_recv, known_send, known_recv,
    lent_send, lent_recv, norm_send, norm_recv,
):
    me = lax.axis_index("tm")
    place = coordinates(me)

    def at(offset):
        return lax.rem(me + offset + count, count)

    loads = [
        pltpu.make_async_copy(src, dst, local_sem.at[n])
        for n, (src, dst) in enumerate(
            (
                (stream, rows.at[pl.ds(TAIL, SHARD)]),
                (weight_hbm, weight),
                (stream.at[pl.ds(SHARD - TAIL, TAIL)], edge.at[pl.ds(2 * EDGE, TAIL)]),
                (stream.at[pl.ds(0, HALO)], edge.at[pl.ds(EDGE + TAIL, HALO)]),
            )
        )
    ]
    for copy in loads:
        copy.start()

    lane = lax.broadcasted_iota(i32, (1, 128), 1)
    line = jnp.zeros((1, 128), f32)
    for j in range(4):
        start = jnp.where(j < live[0], starts[j] // SEG, DEAD).astype(f32)
        line = jnp.where(lane == j, start, line)
        line = jnp.where(lane == 4 + j, profile_index[j].astype(f32), line)
    known[me] = line
    nearby[2] = line

    barrier = pltpu.get_barrier_semaphore()
    partners = [at(offset) for offset in (-2, -1, 1, 2)]
    partners += [lax.div(me, 8) * 8 + lax.rem(me + step, 8) for step in range(1, 8)]
    partners += [lax.rem(me + 8 * step, count) for step in range(1, 16)]
    for k in range(4):
        partners += [helper(place, k), helped(place, k)]
    for partner in partners:
        pl.semaphore_signal(barrier, inc=1, device_id=(partner,), device_id_type=MESH)

    def send(src, dst, send_sem, recv_sem, device):
        copy = pltpu.make_async_remote_copy(
            src_ref=src, dst_ref=dst, send_sem=send_sem, recv_sem=recv_sem, device_id=(device,),
            device_id_type=MESH,
        )
        copy.start()
        return copy

    def tell(first, length, index, device):
        block = known.at[pl.ds(first, length)]
        return send(block, block, known_send.at[index], known_recv.at[index], device)

    def convolved(block, length):
        wide = jnp.concatenate([block[13 + k : 13 + k + length] for k in range(7)], axis=1)
        return gelu32(jnp.dot(wide, weight[...], preferred_element_type=f32) + bias[...])

    def stem(first, length):
        block = rows[pl.ds(first + 32, length + 32)]
        feats[pl.ds(first + HALO, length)] = convolved(block, length).astype(bf16)

    def lend(k):
        return send(
            feats.at[pl.ds(512 * k, 512 + HALO)], lent.at[k], lent_send.at[k], lent_recv.at[k], helper(place, k)
        )

    pl.semaphore_wait(barrier, len(partners))
    edges = [
        send(
            stream.at[pl.ds(SHARD - TAIL, TAIL)], edge.at[pl.ds((2 - offset) * EDGE, TAIL)],
            edge_send.at[index], edge_recv.at[index], at(offset),
        )
        for index, offset in enumerate((2, 1, -1))
    ] + [
        send(
            stream.at[pl.ds(0, HALO)], edge.at[pl.ds((1 - offset) * EDGE + TAIL, HALO)],
            edge_send.at[3 + index], edge_recv.at[3 + index], at(offset),
        )
        for index, offset in enumerate((1, -1, -2))
    ]
    lines = [
        send(known.at[me], nearby.at[2 - offset], line_send.at[index], line_recv.at[index], at(offset))
        for index, offset in enumerate((2, 1, -1))
    ]
    eight = lax.div(me, 8) * 8
    near = [tell(me, 1, step - 1, eight + lax.rem(me + step, 8)) for step in range(1, 8)]
    for copy in loads:
        copy.wait()
    stem(16, 496)
    stem(512, 512)
    stem(1024, 512)
    stem(1536, 496)
    for k in range(NSEG):
        low, high = max(k * SEG, 16), min(k * SEG + SEG, SHARD - 16)
        part = feats[pl.ds(low + HALO, high - low)].astype(f32)
        for n, total in enumerate((part, part * part)):
            total = jnp.sum(total, axis=0, keepdims=True)
            mine[n, k : k + 1] = total
            stats[n, 16 + k : 17 + k] = total
    moments = [
        send(mine, stats.at[:, pl.ds(8 * (2 - offset), 8)], stat_send.at[index], stat_recv.at[index], at(offset))
        for index, offset in enumerate((-2, -1, 1, 2))
    ]
    for copy in near:
        copy.wait()
    far = [tell(eight, 8, 6 + step, lax.rem(me + 8 * step, count)) for step in range(1, 16)]
    for copy in edges:
        copy.wait()
    for b in range(4):

        @pl.when(me - 2 + b == -1)
        def _():
            edge[pl.ds(b * EDGE, TAIL)] = jnp.zeros((TAIL, 128), bf16)

        @pl.when(me - 2 + b == count - 1)
        def _():
            edge[pl.ds(b * EDGE + TAIL, HALO)] = jnp.zeros((HALO, 128), bf16)

    rows[pl.ds(0, TAIL)] = edge[pl.ds(EDGE, TAIL)]
    rows[pl.ds(SHARD + TAIL, 16)] = edge[pl.ds(2 * EDGE + TAIL, 16)]
    stem(-HALO, HALO + 16)
    stem(SHARD - 16, 16)
    loans = [lend(k) for k in range(4)]
    ends = convolved(edge[...], 4 * EDGE - 32).astype(bf16).astype(f32)
    for copy in moments + lines:
        copy.wait()
    for b in range(4):
        for side in range(2):
            part = ends[b * EDGE + 16 * (1 + side) : b * EDGE + 16 * (2 + side)]
            row = 8 * b + 7 + side
            stats[0, row : row + 1] += jnp.sum(part, axis=0, keepdims=True)
            stats[1, row : row + 1] += jnp.sum(part * part, axis=0, keepdims=True)

    row = lax.broadcasted_iota(i32, (40, 128), 0).astype(f32)
    for slot in range(SLOTS):
        start = nearby[slot // 4][:, slot % 4 : slot % 4 + 1]
        first = start - (NSEG * me - 16).astype(f32)
        covered = jnp.logical_and(row >= first, row < first + WSEG)
        mean, square = (
            jnp.sum(jnp.where(covered, stats[n], 0.0), axis=0, keepdims=True) * (1.0 / (WSEG * SEG))
            for n in range(2)
        )
        scale = lax.rsqrt(square - mean * mean + EPS)
        norms[slot : slot + 1] = scale
        norms[SLOTS + slot : SLOTS + slot + 1] = -mean * scale
    for k in range(4):
        loans.append(send(norms, lent_norms.at[k], norm_send.at[k], norm_recv.at[k], helper(place, k)))

    for copy in far:
        copy.wait()
    turned = known[...].reshape(128, 128).T[:8]
    table[...] = turned.astype(i32)
    given = share_out(turned)
    shares[...] = jnp.concatenate([given[k][:1] for k in range(4)] + [jnp.zeros((4, 128), f32)], axis=0).astype(i32)
    for copy in loans:
        copy.wait()


def make_features(count, starts, profile_index, counts, stream, weight, bias):
    vmem, smem, hbm = (pl.BlockSpec(memory_space=m) for m in (pltpu.VMEM, pltpu.SMEM, pl.ANY))
    dma = pltpu.SemaphoreType.DMA
    return pl.pallas_call(
        functools.partial(feature_kernel, count),
        out_shape=[
            jax.ShapeDtypeStruct((SHARD + HALO, 128), bf16),
            jax.ShapeDtypeStruct((2 * SLOTS, 128), f32),
            jax.ShapeDtypeStruct((8, 128), i32),
            jax.ShapeDtypeStruct((8, 128), i32),
            jax.ShapeDtypeStruct((4, 512 + HALO, 128), bf16),
            jax.ShapeDtypeStruct((4, 2 * SLOTS, 128), f32),
        ],
        in_specs=[smem, smem, smem, hbm, hbm, vmem],
        out_specs=[vmem, vmem, vmem, vmem, hbm, hbm],
        scratch_shapes=[
            pltpu.VMEM((SHARD + 64, 128), bf16),
            pltpu.VMEM((7 * 128, 128), bf16),
            pltpu.VMEM((2, 40, 128), f32),
            pltpu.VMEM((2, NSEG, 128), f32),
            pltpu.VMEM((128, 1, 128), f32),
            pltpu.VMEM((5, 1, 128), f32),
            pltpu.VMEM((4 * EDGE, 128), bf16),
            dma((4,)),
            dma((6,)), dma((6,)),
            dma((3,)), dma((3,)),
            dma((4,)), dma((4,)),
            dma((22,)), dma((22,)),
            dma((4,)), dma((4,)),
            dma((4,)), dma((4,)),
        ],
        compiler_params=pltpu.CompilerParams(
            collective_id=0, has_side_effects=True, vmem_limit_bytes=56 * 2**20
        ),
    )(starts, profile_index, counts, stream, weight, bias)


BIG = 2048
CAPACITY = 128 * SEG + 128 * HALO + BIG
UNITS = 160


def network_kernel(
    count, table, shares, feats_hbm, lent_hbm, norms_hbm, lent_norms_hbm, first_hbm, deep_hbm, layer_bias, head_hbm,
    head_bias, profiles, sums, lent_sums, feats, norms, first_weight, deep_weight, head_weight, x_stack, h_a,
    h_b, total, head_turned, padded, weights, unit, zeros, sems,
):
    me = lax.axis_index("tm")
    place = coordinates(me)
    pieces = [
        (first_hbm, first_weight),
        (deep_hbm, deep_weight),
        (head_hbm, head_weight),
        (feats_hbm, feats.at[pl.ds(0, SHARD + HALO)]),
        (norms_hbm, norms.at[pl.ds(0, 2 * SLOTS)]),
    ]
    for k in range(4):
        pieces.append((lent_hbm.at[k], feats.at[pl.ds(SHARD + HALO + (512 + HALO) * k, 512 + HALO)]))
        pieces.append((lent_norms_hbm.at[k], norms.at[pl.ds(2 * SLOTS * (k + 1), 2 * SLOTS)]))
    loads = [pltpu.make_async_copy(src, dst, sems.at[n]) for n, (src, dst) in enumerate(pieces)]
    for copy in loads[3:] + loads[:3]:
        copy.start()

    padded[...] = jnp.zeros_like(padded)
    for p in range(4):
        for k in range(WSEG):
            padded[p * 32 + 8 + k : p * 32 + 9 + k] = profiles[p : p + 1, k * SEG : (k + 1) * SEG]
    weights[...] = jnp.zeros_like(weights)

    def clear(index, carry):
        total[:, pl.ds(pl.multiple_of(index * SEG, SEG), SEG)] = jnp.zeros((128, SEG), f32)
        return carry

    lax.fori_loop(0, 2 * NSEG, clear, 0)
    for copy in loads[3:]:
        copy.wait()

    def window(home, slot):
        owner = home + slot // 4 - 2
        inside = jnp.logical_and(owner >= 0, owner < count)
        owner = jnp.clip(owner, 0, count - 1)
        start = jnp.where(inside, table[lax.rem(slot, 4), owner], DEAD)
        return start - NSEG * home, table[4 + lax.rem(slot, 4), owner]

    def put(base, target, norm, slot, rel, profile, low, high, fresh, state):
        scale = norms[pl.ds(norm + slot, 1)]
        shift = norms[pl.ds(norm + SLOTS + slot, 1)]

        def normalised(row, length):
            block = feats[pl.ds(pl.multiple_of(row, 32), length)].astype(f32)
            return (block * scale + shift).astype(bf16)

        def begin(state):
            rows, units, blanks = state
            rows = pl.multiple_of(rows, 32)

            @pl.when(low == rel)
            def _():
                x_stack[pl.ds(rows + HALO, HALO)] = jnp.zeros((HALO, 128), bf16)
                zeros[blanks] = rows + HALO

            @pl.when(low != rel)
            def _():
                x_stack[pl.ds(rows + HALO, HALO)] = normalised(base + low * SEG, HALO)

            return rows + HALO, units, blanks + jnp.where(low == rel, 1, 0)

        def segment(k, state):
            rows, units, blanks = state
            rows = pl.multiple_of(rows, 32)
            x_stack[pl.ds(rows + HALO, SEG)] = normalised(base + k * SEG + HALO, SEG)
            unit[0, units] = rows
            unit[1, units] = target + k * SEG
            unit[2, units] = profile * 32 + 8 + k - rel
            return rows + SEG, units + 1, blanks

        state = lax.cond(fresh, begin, lambda s: s, state)
        return lax.fori_loop(low, high, segment, state)

    def own_slot(slot, carry):
        rel, profile = window(me, slot)

        def covered(carry):
            for k in range(NSEG):
                weights[k : k + 1] += padded[pl.ds(profile * 32 + 8 - rel + k, 1)]
            state, lefts = carry[:3], list(carry[3:])
            end = i32(-1)
            for k in range(4):
                first = jnp.maximum(rel, 2 * k)
                high = jnp.minimum(rel + WSEG, 2 * k + 2)
                given = jnp.minimum(lefts[k], jnp.maximum(high - first, 0))
                lefts[k] = lefts[k] - given
                low = first + given
                fresh = jnp.logical_and(high > low, low != end)
                state = put(0, 0, 0, slot, rel, profile, low, high, fresh, state)
                end = jnp.where(high > low, high, end)
            return (*state, *lefts)

        return lax.cond(jnp.logical_and(rel > -WSEG, rel < NSEG), covered, lambda c: c, carry)

    carry = lax.fori_loop(0, SLOTS, own_slot, (i32(0), i32(0), i32(0), *(shares[k, me] for k in range(4))))
    state = carry[:3]
    for k in range(4):
        home = helped(place, k)
        share = shares[k, home]

        def lent_slot(slot, carry, k=k, home=home):
            rel, profile = window(home, slot)

            def covered(carry):
                for i in range(2):
                    row = NSEG + 2 * k + i
                    weights[row : row + 1] += padded[pl.ds(profile * 32 + 8 - rel + 2 * k + i, 1)]
                first = jnp.maximum(rel, 2 * k)
                taken = jnp.minimum(carry[3], jnp.maximum(jnp.minimum(rel + WSEG, 2 * k + 2) - first, 0))
                state = put(
                    SHARD + HALO + HALO * k, SHARD, 2 * SLOTS * (k + 1), slot, rel, profile, first, first + taken,
                    taken > 0, carry[:3],
                )
                return (*state, carry[3] - taken)

            return lax.cond(jnp.logical_and(rel > -WSEG, rel < NSEG), covered, lambda c: c, carry)

        state = lax.fori_loop(0, jnp.where(share > 0, SLOTS, 0), lent_slot, (*state, share))[:3]
    rows, units, blanks = state

    for copy in loads[:3]:
        copy.wait()
    sizes, spans, first = (2048, 1024, 512), [], i32(0)
    for size in sizes:
        steps = (rows - first + (size - 1 if size == sizes[-1] else 0)) // size
        spans.append((size, first, steps))
        first = first + steps * size

    def over_rows(body):
        for size, first, steps in spans:

            def step(index, carry, size=size, first=first):
                body(pl.multiple_of(first + index * size, sizes[-1]), size)
                return carry

            lax.fori_loop(0, steps, step, 0)

    def layer(index, source, target, weight):
        spread = 2**index

        def body(first, length):
            block = source[pl.ds(first, length + HALO)]
            wide = jnp.concatenate(
                [block[HALO - s * spread : HALO - s * spread + length] for s in (2, 1, 0)], axis=1
            )
            summed = jnp.dot(wide, weight, preferred_element_type=f32)
            made = gelu16(summed + layer_bias[index : index + 1])
            if index:
                made = made + block[HALO:]
            target[pl.ds(first + HALO, length)] = made

        over_rows(body)

        def blank(n, carry):
            target[pl.ds(pl.multiple_of(zeros[n], 32), HALO)] = jnp.zeros((HALO, 256), bf16)
            return carry

        lax.fori_loop(0, blanks, blank, 0)

    layer(0, x_stack, h_a, first_weight[...])
    layer(1, h_a, h_b, deep_weight[0])
    layer(2, h_b, h_a, deep_weight[1])
    layer(3, h_a, h_b, deep_weight[2])

    for extra in range(3):
        unit[0, units + extra] = unit[0, 0]
        unit[1, units + extra] = 0
        unit[2, units + extra] = 0

    for half in range(2):
        part = head_weight[pl.ds(half * 128, 128)].astype(f32)
        head_turned[:, half * 128 : (half + 1) * 128] = part.T.astype(bf16)

    def gather(n, carry):
        for u in range(4):
            rows = pl.multiple_of(unit[0, 4 * n + u] + HALO, 32)
            target = pl.ds(pl.multiple_of(unit[1, 4 * n + u], SEG), SEG)
            made = lax.dot_general(
                head_turned[...], h_b[pl.ds(rows, SEG)], (((1,), (1,)), ((), ())), preferred_element_type=f32
            )
            total[:, target] += made * padded[pl.ds(unit[2, 4 * n + u], 1)]
        return carry

    lax.fori_loop(0, (units + 3) // 4, gather, 0)

    bias = jnp.broadcast_to(head_bias[...], (8, 128)).T[:, :1]

    def store(index, carry):
        mine, lent = pl.ds(pl.multiple_of(index * SEG, SEG), SEG), pl.multiple_of(SHARD + index * SEG, SEG)
        weight = weights[pl.ds(index, 1)]
        made = (total[:, mine] + bias * weight) * (1.0 / jnp.maximum(weight, 1.0))
        sums[mine] = made.T.astype(bf16)
        weight = weights[pl.ds(NSEG + index, 1)]
        made = total[:, pl.ds(lent, SEG)] * (1.0 / jnp.maximum(weight, 1.0))
        lent_sums[mine] = made.T.astype(bf16)
        return carry

    lax.fori_loop(0, NSEG, store, 0)


def run_network(count, table, shares, feats, lent, norms, lent_norms, net, profiles):
    vmem, smem, hbm = (pl.BlockSpec(memory_space=m) for m in (pltpu.VMEM, pltpu.SMEM, pl.ANY))
    first_weight, deep_weight, layer_bias, head_weight, head_bias = net
    return pl.pallas_call(
        functools.partial(network_kernel, count),
        out_shape=[
            jax.ShapeDtypeStruct((SHARD, 128), bf16),
            jax.ShapeDtypeStruct((SHARD, 128), bf16),
        ],
        in_specs=[smem, smem, hbm, hbm, hbm, hbm, hbm, hbm, vmem, hbm, vmem, vmem],
        out_specs=[vmem, vmem],
        scratch_shapes=[
            pltpu.VMEM((SHARD + HALO + 4 * (512 + HALO), 128), bf16),
            pltpu.VMEM((10 * SLOTS, 128), f32),
            pltpu.VMEM((384, 256), bf16),
            pltpu.VMEM((3, 768, 256), bf16),
            pltpu.VMEM((256, 128), bf16),
            pltpu.VMEM((CAPACITY + HALO, 128), bf16),
            pltpu.VMEM((CAPACITY + HALO, 256), bf16),
            pltpu.VMEM((CAPACITY + HALO, 256), bf16),
            pltpu.VMEM((128, 2 * SHARD), f32),
            pltpu.VMEM((128, 256), bf16),
            pltpu.VMEM((4 * 32, SEG), f32),
            pltpu.VMEM((2 * NSEG, SEG), f32),
            pltpu.SMEM((3, UNITS), i32),
            pltpu.SMEM((UNITS,), i32),
            pltpu.SemaphoreType.DMA((13,)),
        ],
        compiler_params=pltpu.CompilerParams(vmem_limit_bytes=62 * 2**20),
    )(table, shares, feats, lent, norms, lent_norms, first_weight, deep_weight, layer_bias, head_weight, head_bias, profiles)


def return_kernel(lent_sums, arrived, send_sem, recv_sem):
    me = lax.axis_index("tm")
    place = coordinates(me)
    barrier = pltpu.get_barrier_semaphore()
    for k in range(4):
        for partner in (helper(place, k), helped(place, k)):
            pl.semaphore_signal(barrier, inc=1, device_id=(partner,), device_id_type=MESH)
    pl.semaphore_wait(barrier, 8)
    copies = []
    for k in range(4):
        rows = pl.ds(512 * k, 512)
        copy = pltpu.make_async_remote_copy(
            src_ref=lent_sums.at[rows], dst_ref=arrived.at[rows], send_sem=send_sem.at[k], recv_sem=recv_sem.at[k],
            device_id=(helped(place, k),), device_id_type=MESH,
        )
        copy.start()
        copies.append(copy)
    for copy in copies:
        copy.wait()


def bring_back(lent_sums):
    hbm = pl.BlockSpec(memory_space=pl.ANY)
    return pl.pallas_call(
        return_kernel,
        out_shape=jax.ShapeDtypeStruct((SHARD, 128), bf16),
        in_specs=[hbm],
        out_specs=hbm,
        scratch_shapes=[pltpu.SemaphoreType.DMA((4,)), pltpu.SemaphoreType.DMA((4,))],
        compiler_params=pltpu.CompilerParams(
            collective_id=1, has_side_effects=True, vmem_limit_bytes=56 * 2**20
        ),
    )(lent_sums)


def per_device(
    stream, stem_weight, stem_bias, first_weight, deep_weight, layer_bias, head_weight, head_bias,
    profiles, starts, profile_index, counts,
):
    count = lax.axis_size("tm")
    feats, norms, table, shares, lent, lent_norms = make_features(
        count, starts, profile_index, counts, stream, stem_weight.reshape(7 * 128, 128), stem_bias.reshape(1, 128)
    )
    net = (
        first_weight.reshape(3 * 128, 256),
        deep_weight.reshape(3, 3 * 256, 256),
        layer_bias,
        head_weight,
        head_bias.reshape(1, 128),
    )
    sums, lent_sums = run_network(count, table, shares, feats, lent, norms, lent_norms, net, profiles)
    return (sums.astype(f32) + bring_back(lent_sums).astype(f32)).astype(bf16)


def solution(mesh):
    in_specs = (P("tm", None), P(), P(), P(), P(), P(), P(), P(), P(), P("tm"), P("tm"), P("tm"))
    return jax.shard_map(
        per_device, mesh=mesh, in_specs=in_specs, out_specs=P("tm", None), check_vma=False
    )
```

```python
import functools
import math

import jax
import jax.numpy as jnp
from jax import lax
from jax.experimental import pallas as pl
from jax.experimental.pallas import tpu as pltpu
from jax.sharding import PartitionSpec as P

bf16, f32, i32 = jnp.bfloat16, jnp.float32, jnp.int32
MESH = pl.DeviceIdType.MESH
EPS = 1e-05
SEG = 256
HALO = 32
WSEG = 16
SWEEPS = 3
SHARD = 2048
NSEG = SHARD // SEG
SLOTS = 16
TAIL = 48
EDGE = TAIL + HALO
DEAD = -100000
G1 = math.sqrt(2.0 / math.pi)
G2 = G1 * 0.044715


def gelu32(v):
    half = 0.5 * v
    return half + half * jnp.tanh(v * (G1 + G2 * (v * v)))


def gelu16(v):
    v = v.astype(bf16)
    half = bf16(0.5) * v
    return half + half * jnp.tanh(v * (bf16(G1) + bf16(G2) * (v * v)))


def coordinates(d):
    return lax.div(d, 32), lax.rem(lax.div(d, 8), 4), lax.rem(lax.div(d, 2), 4), lax.rem(d, 2)


def device_at(y, z, x, core):
    return y * 32 + z * 8 + x * 2 + core


def helper(place, k):
    y, z, x, core = place
    if k == 0:
        return device_at(lax.rem(y + 1, 4), z, x, 1 - core)
    if k == 1:
        return device_at(lax.rem(y + 3, 4), z, x, core)
    if k == 2:
        return device_at(y, lax.rem(z + 1, 4), x, 1 - core)
    return device_at(y, lax.rem(z + 3, 4), x, core)


def helped(place, k):
    y, z, x, core = place
    if k == 0:
        return device_at(lax.rem(y + 3, 4), z, x, 1 - core)
    if k == 1:
        return device_at(lax.rem(y + 1, 4), z, x, core)
    if k == 2:
        return device_at(y, lax.rem(z + 3, 4), x, 1 - core)
    return device_at(y, lax.rem(z + 1, 4), x, core)


def lanes_core(v, lane):
    return jnp.where(lane % 2 == 0, pltpu.roll(v, 127, 1), pltpu.roll(v, 1, 1))


def lanes_y(v, lane, step):
    return pltpu.roll(v, 96 if step > 0 else 32, 1)


def lanes_z(v, lane, step):
    if step > 0:
        return jnp.where(lane % 32 < 24, pltpu.roll(v, 120, 1), pltpu.roll(v, 24, 1))
    return jnp.where(lane % 32 >= 8, pltpu.roll(v, 8, 1), pltpu.roll(v, 104, 1))


def at_helper(v, lane, k):
    if k == 0:
        return lanes_y(lanes_core(v, lane), lane, 1)
    if k == 1:
        return lanes_y(v, lane, -1)
    if k == 2:
        return lanes_z(lanes_core(v, lane), lane, 1)
    return lanes_z(v, lane, -1)


def at_helped(v, lane, k):
    if k == 0:
        return lanes_core(lanes_y(v, lane, -1), lane)
    if k == 1:
        return lanes_y(v, lane, 1)
    if k == 2:
        return lanes_core(lanes_z(v, lane, -1), lane)
    return lanes_z(v, lane, 1)


def share_out(rows):
    lane = lax.broadcasted_iota(i32, (8, 128), 1)
    segment = (lane * NSEG + lax.broadcasted_iota(i32, (8, 128), 0)).astype(f32)
    covering = jnp.zeros((8, 128), f32)
    for j in range(4):
        start = jnp.broadcast_to(rows[j : j + 1], (8, 128))
        for offset in range(-2, 2):
            moved = pltpu.roll(start, (-offset) % 128, 1) if offset else start
            there = jnp.logical_and(lane + offset >= 0, lane + offset < 128)
            there = jnp.logical_and(there, jnp.logical_and(segment >= moved, segment < moved + WSEG))
            covering = covering + jnp.where(there, 1.0, 0.0)
    caps = [
        jnp.broadcast_to(covering[2 * k : 2 * k + 1] + covering[2 * k + 1 : 2 * k + 2], (8, 128))
        for k in range(4)
    ]
    load = caps[0] + caps[1] + caps[2] + caps[3]
    given = [jnp.zeros((8, 128), f32) for _ in range(4)]
    for _ in range(SWEEPS):
        for k in range(4):
            half = 0.5 * (load - at_helper(load, lane, k))
            move = jnp.where(half >= 0, jnp.floor(half), -jnp.floor(-half))
            move = jnp.clip(move, -given[k], caps[k] - given[k])
            given[k] = given[k] + move
            load = load - move + at_helped(move, lane, k)
    return given


def feature_kernel(
    count, starts, profile_index, live, stream, weight_hbm, bias, feats, norms, table, shares, lent, lent_norms,
    rows, weight, stats, mine, known, nearby, edge, local_sem, edge_send, edge_recv, line_send, line_recv, stat_send,
    stat_recv, known_send, known_recv,
    lent_send, lent_recv, norm_send, norm_recv,
):
    me = lax.axis_index("tm")
    place = coordinates(me)

    def at(offset):
        return lax.rem(me + offset + count, count)

    loads = [
        pltpu.make_async_copy(src, dst, local_sem.at[n])
        for n, (src, dst) in enumerate(
            (
                (stream, rows.at[pl.ds(TAIL, SHARD)]),
                (weight_hbm, weight),
                (stream.at[pl.ds(SHARD - TAIL, TAIL)], edge.at[pl.ds(2 * EDGE, TAIL)]),
                (stream.at[pl.ds(0, HALO)], edge.at[pl.ds(EDGE + TAIL, HALO)]),
            )
        )
    ]
    for copy in loads:
        copy.start()

    lane = lax.broadcasted_iota(i32, (1, 128), 1)
    line = jnp.zeros((1, 128), f32)
    for j in range(4):
        start = jnp.where(j < live[0], starts[j] // SEG, DEAD).astype(f32)
        line = jnp.where(lane == j, start, line)
        line = jnp.where(lane == 4 + j, profile_index[j].astype(f32), line)
    known[me] = line
    nearby[2] = line

    barrier = pltpu.get_barrier_semaphore()
    partners = [at(offset) for offset in (-2, -1, 1, 2)]
    partners += [lax.div(me, 8) * 8 + lax.rem(me + step, 8) for step in range(1, 8)]
    partners += [lax.rem(me + 8 * step, count) for step in range(1, 16)]
    for k in range(4):
        partners += [helper(place, k), helped(place, k)]
    for partner in partners:
        pl.semaphore_signal(barrier, inc=1, device_id=(partner,), device_id_type=MESH)

    def send(src, dst, send_sem, recv_sem, device):
        copy = pltpu.make_async_remote_copy(
            src_ref=src, dst_ref=dst, send_sem=send_sem, recv_sem=recv_sem, device_id=(device,),
            device_id_type=MESH,
        )
        copy.start()
        return copy

    def tell(first, length, index, device):
        block = known.at[pl.ds(first, length)]
        return send(block, block, known_send.at[index], known_recv.at[index], device)

    def convolved(block, length):
        wide = jnp.concatenate([block[13 + k : 13 + k + length] for k in range(7)], axis=1)
        return gelu32(jnp.dot(wide, weight[...], preferred_element_type=f32) + bias[...])

    def stem(first, length):
        block = rows[pl.ds(first + 32, length + 32)]
        feats[pl.ds(first + HALO, length)] = convolved(block, length).astype(bf16)

    def lend(k):
        return send(
            feats.at[pl.ds(512 * k, 512 + HALO)], lent.at[k], lent_send.at[k], lent_recv.at[k], helper(place, k)
        )

    pl.semaphore_wait(barrier, len(partners))
    edges = [
        send(
            stream.at[pl.ds(SHARD - TAIL, TAIL)], edge.at[pl.ds((2 - offset) * EDGE, TAIL)],
            edge_send.at[index], edge_recv.at[index], at(offset),
        )
        for index, offset in enumerate((2, 1, -1))
    ] + [
        send(
            stream.at[pl.ds(0, HALO)], edge.at[pl.ds((1 - offset) * EDGE + TAIL, HALO)],
            edge_send.at[3 + index], edge_recv.at[3 + index], at(offset),
        )
        for index, offset in enumerate((1, -1, -2))
    ]
    lines = [
        send(known.at[me], nearby.at[2 - offset], line_send.at[index], line_recv.at[index], at(offset))
        for index, offset in enumerate((2, 1, -1))
    ]
    eight = lax.div(me, 8) * 8
    near = [tell(me, 1, step - 1, eight + lax.rem(me + step, 8)) for step in range(1, 8)]
    for copy in loads:
        copy.wait()
    stem(16, 496)
    stem(512, 512)
    stem(1024, 512)
    stem(1536, 496)
    for k in range(NSEG):
        low, high = max(k * SEG, 16), min(k * SEG + SEG, SHARD - 16)
        part = feats[pl.ds(low + HALO, high - low)].astype(f32)
        for n, total in enumerate((part, part * part)):
            total = jnp.sum(total, axis=0, keepdims=True)
            mine[n, k : k + 1] = total
            stats[n, 16 + k : 17 + k] = total
    moments = [
        send(mine, stats.at[:, pl.ds(8 * (2 - offset), 8)], stat_send.at[index], stat_recv.at[index], at(offset))
        for index, offset in enumerate((-2, -1, 1, 2))
    ]
    for copy in near:
        copy.wait()
    far = [tell(eight, 8, 6 + step, lax.rem(me + 8 * step, count)) for step in range(1, 16)]
    for copy in edges:
        copy.wait()
    for b in range(4):

        @pl.when(me - 2 + b == -1)
        def _():
            edge[pl.ds(b * EDGE, TAIL)] = jnp.zeros((TAIL, 128), bf16)

        @pl.when(me - 2 + b == count - 1)
        def _():
            edge[pl.ds(b * EDGE + TAIL, HALO)] = jnp.zeros((HALO, 128), bf16)

    rows[pl.ds(0, TAIL)] = edge[pl.ds(EDGE, TAIL)]
    rows[pl.ds(SHARD + TAIL, 16)] = edge[pl.ds(2 * EDGE + TAIL, 16)]
    stem(-HALO, HALO + 16)
    stem(SHARD - 16, 16)
    loans = [lend(k) for k in range(4)]
    ends = convolved(edge[...], 4 * EDGE - 32).astype(bf16).astype(f32)
    for copy in moments + lines:
        copy.wait()
    for b in range(4):
        for side in range(2):
            part = ends[b * EDGE + 16 * (1 + side) : b * EDGE + 16 * (2 + side)]
            row = 8 * b + 7 + side
            stats[0, row : row + 1] += jnp.sum(part, axis=0, keepdims=True)
            stats[1, row : row + 1] += jnp.sum(part * part, axis=0, keepdims=True)

    row = lax.broadcasted_iota(i32, (40, 128), 0).astype(f32)
    for slot in range(SLOTS):
        start = nearby[slot // 4][:, slot % 4 : slot % 4 + 1]
        first = start - (NSEG * me - 16).astype(f32)
        covered = jnp.logical_and(row >= first, row < first + WSEG)
        mean, square = (
            jnp.sum(jnp.where(covered, stats[n], 0.0), axis=0, keepdims=True) * (1.0 / (WSEG * SEG))
            for n in range(2)
        )
        scale = lax.rsqrt(square - mean * mean + EPS)
        norms[slot : slot + 1] = scale
        norms[SLOTS + slot : SLOTS + slot + 1] = -mean * scale
    for k in range(4):
        loans.append(send(norms, lent_norms.at[k], norm_send.at[k], norm_recv.at[k], helper(place, k)))

    for copy in far:
        copy.wait()
    turned = known[...].reshape(128, 128).T[:8]
    table[...] = turned.astype(i32)
    given = share_out(turned)
    shares[...] = jnp.concatenate([given[k][:1] for k in range(4)] + [jnp.zeros((4, 128), f32)], axis=0).astype(i32)
    for copy in loans:
        copy.wait()


def make_features(count, starts, profile_index, counts, stream, weight, bias):
    vmem, smem, hbm = (pl.BlockSpec(memory_space=m) for m in (pltpu.VMEM, pltpu.SMEM, pl.ANY))
    dma = pltpu.SemaphoreType.DMA
    return pl.pallas_call(
        functools.partial(feature_kernel, count),
        out_shape=[
            jax.ShapeDtypeStruct((SHARD + HALO, 128), bf16),
            jax.ShapeDtypeStruct((2 * SLOTS, 128), f32),
            jax.ShapeDtypeStruct((8, 128), i32),
            jax.ShapeDtypeStruct((8, 128), i32),
            jax.ShapeDtypeStruct((4, 512 + HALO, 128), bf16),
            jax.ShapeDtypeStruct((4, 2 * SLOTS, 128), f32),
        ],
        in_specs=[smem, smem, smem, hbm, hbm, vmem],
        out_specs=[vmem, vmem, vmem, vmem, hbm, hbm],
        scratch_shapes=[
            pltpu.VMEM((SHARD + 64, 128), bf16),
            pltpu.VMEM((7 * 128, 128), bf16),
            pltpu.VMEM((2, 40, 128), f32),
            pltpu.VMEM((2, NSEG, 128), f32),
            pltpu.VMEM((128, 1, 128), f32),
            pltpu.VMEM((5, 1, 128), f32),
            pltpu.VMEM((4 * EDGE, 128), bf16),
            dma((4,)),
            dma((6,)), dma((6,)),
            dma((3,)), dma((3,)),
            dma((4,)), dma((4,)),
            dma((22,)), dma((22,)),
            dma((4,)), dma((4,)),
            dma((4,)), dma((4,)),
        ],
        compiler_params=pltpu.CompilerParams(
            collective_id=0, has_side_effects=True, vmem_limit_bytes=56 * 2**20
        ),
    )(starts, profile_index, counts, stream, weight, bias)


SIZES = (4608, 2304, 1152, 576)
BATCH = 48
CAPACITY = -(-BATCH * (SEG + HALO) // SIZES[-1]) * SIZES[-1]
UNITS = 136


def network_kernel(
    count, table, shares, feats_hbm, lent_hbm, norms_hbm, lent_norms_hbm, first_hbm, deep_hbm, layer_bias, head_hbm,
    head_bias, profiles, sums, lent_sums, feats, norms, first_weight, deep_weight, head_weight, x_stack, h_a,
    h_b, total, head_turned, padded, weights, unit, zeros, sems,
):
    me = lax.axis_index("tm")
    place = coordinates(me)
    pieces = [
        (first_hbm, first_weight),
        (deep_hbm, deep_weight),
        (head_hbm, head_weight),
        (feats_hbm, feats.at[pl.ds(0, SHARD + HALO)]),
        (norms_hbm, norms.at[pl.ds(0, 2 * SLOTS)]),
    ]
    for k in range(4):
        pieces.append((lent_hbm.at[k], feats.at[pl.ds(SHARD + HALO + (512 + HALO) * k, 512 + HALO)]))
        pieces.append((lent_norms_hbm.at[k], norms.at[pl.ds(2 * SLOTS * (k + 1), 2 * SLOTS)]))
    loads = [pltpu.make_async_copy(src, dst, sems.at[n]) for n, (src, dst) in enumerate(pieces)]
    for copy in loads[3:] + loads[:3]:
        copy.start()

    padded[...] = jnp.zeros_like(padded)
    for p in range(4):
        for k in range(WSEG):
            padded[p * 32 + 8 + k : p * 32 + 9 + k] = profiles[p : p + 1, k * SEG : (k + 1) * SEG]
    weights[...] = jnp.zeros_like(weights)

    def clear(index, carry):
        total[:, pl.ds(pl.multiple_of(index * SEG, SEG), SEG)] = jnp.zeros((128, SEG), f32)
        return carry

    lax.fori_loop(0, 2 * NSEG, clear, 0)

    def window(home, slot):
        owner = home + slot // 4 - 2
        inside = jnp.logical_and(owner >= 0, owner < count)
        owner = jnp.clip(owner, 0, count - 1)
        start = jnp.where(inside, table[lax.rem(slot, 4), owner], DEAD)
        return start - NSEG * home, table[4 + lax.rem(slot, 4), owner]

    def put(base, target, norm, rel, profile, low, high, fresh, state):
        def segment(k, state):
            rows, units = state
            ahead = jnp.where(jnp.logical_and(k == low, fresh), jnp.where(k == rel, 2, 1), 0)
            rows = rows + jnp.where(ahead > 0, HALO, 0)
            unit[0, units] = rows
            unit[1, units] = target + k * SEG
            unit[2, units] = profile * 32 + 8 + k - rel
            unit[3, units] = base + k * SEG
            unit[4, units] = norm
            unit[5, units] = ahead
            return rows + SEG, units + 1

        return lax.fori_loop(low, high, segment, state)

    def own_slot(slot, carry):
        rel, profile = window(me, slot)

        def covered(carry):
            for k in range(NSEG):
                weights[k : k + 1] += padded[pl.ds(profile * 32 + 8 - rel + k, 1)]
            state, lefts = carry[:2], list(carry[2:])
            end = i32(-1)
            for k in range(4):
                first = jnp.maximum(rel, 2 * k)
                high = jnp.minimum(rel + WSEG, 2 * k + 2)
                given = jnp.minimum(lefts[k], jnp.maximum(high - first, 0))
                lefts[k] = lefts[k] - given
                low = first + given
                state = put(0, 0, slot, rel, profile, low, high, low != end, state)
                end = jnp.where(high > low, high, end)
            return (*state, *lefts)

        return lax.cond(jnp.logical_and(rel > -WSEG, rel < NSEG), covered, lambda c: c, carry)

    carry = lax.fori_loop(0, SLOTS, own_slot, (i32(0), i32(0), *(shares[k, me] for k in range(4))))
    state = carry[:2]
    for k in range(4):
        home = helped(place, k)
        share = shares[k, home]

        def lent_slot(slot, carry, k=k, home=home):
            rel, profile = window(home, slot)

            def covered(carry):
                for i in range(2):
                    row = NSEG + 2 * k + i
                    weights[row : row + 1] += padded[pl.ds(profile * 32 + 8 - rel + 2 * k + i, 1)]
                first = jnp.maximum(rel, 2 * k)
                taken = jnp.minimum(carry[2], jnp.maximum(jnp.minimum(rel + WSEG, 2 * k + 2) - first, 0))
                state = put(
                    SHARD + HALO + HALO * k, SHARD, SLOTS * (k + 1) + slot, rel, profile, first, first + taken,
                    True, carry[:2],
                )
                return (*state, carry[2] - taken)

            return lax.cond(jnp.logical_and(rel > -WSEG, rel < NSEG), covered, lambda c: c, carry)

        state = lax.fori_loop(0, jnp.where(share > 0, SLOTS, 0), lent_slot, (*state, share))[:2]
    rows, units = state
    unit[0, units] = rows + HALO

    for copy in loads:
        copy.wait()
    for half in range(2):
        part = head_weight[pl.ds(half * 128, 128)].astype(f32)
        head_turned[:, half * 128 : (half + 1) * 128] = part.T.astype(bf16)

    def batch(b, carry):
        begin, end = b * BATCH, jnp.minimum(b * BATCH + BATCH, units)
        shift = unit[0, begin] - HALO

        def fill(n, blanks):
            first = pl.multiple_of(unit[0, n] - shift, 32)
            norm, source = unit[4, n], pl.multiple_of(unit[3, n], 32)
            scale = norms[pl.ds(norm // SLOTS * 2 * SLOTS + norm % SLOTS, 1)]
            offset = norms[pl.ds(norm // SLOTS * 2 * SLOTS + SLOTS + norm % SLOTS, 1)]
            ahead = jnp.where(jnp.logical_and(n == begin, unit[5, n] == 0), 1, unit[5, n])

            def normalised(row, length):
                return (feats[pl.ds(row, length)].astype(f32) * scale + offset).astype(bf16)

            x_stack[pl.ds(first + HALO, SEG)] = normalised(pl.multiple_of(source + HALO, 32), SEG)

            @pl.when(ahead == 1)
            def _():
                x_stack[pl.ds(first, HALO)] = normalised(source, HALO)

            @pl.when(ahead == 2)
            def _():
                x_stack[pl.ds(first, HALO)] = jnp.zeros((HALO, 128), bf16)
                zeros[blanks] = first

            return blanks + jnp.where(ahead == 2, 1, 0)

        blanks = lax.fori_loop(begin, end, fill, i32(0))
        rows = unit[0, end - 1] - shift + SEG
        spans, first = [], i32(0)
        for size in SIZES:
            steps = (rows - first + (size - 1 if size == SIZES[-1] else 0)) // size
            spans.append((size, first, steps))
            first = first + steps * size
        run_batch(begin, end, shift, spans, blanks)
        return carry

    def run_batch(begin, end, shift, spans, blanks):
        def over_rows(body):
            for size, first, steps in spans:

                def step(index, carry, size=size, first=first):
                    body(pl.multiple_of(first + index * size, SIZES[-1]), size)
                    return carry

                lax.fori_loop(0, steps, step, 0)

        def layer(index, source, target, weight):
            spread = 2**index

            def body(first, length):
                block = source[pl.ds(first, length + HALO)]
                width, summed = block.shape[1], layer_bias[index : index + 1]
                for tap in range(3):
                    at = HALO - (2 - tap) * spread
                    part = weight[tap * width : (tap + 1) * width]
                    summed = summed + jnp.dot(block[at : at + length], part, preferred_element_type=f32)
                made = gelu16(summed)
                if index:
                    made = made + block[HALO:]
                target[pl.ds(first + HALO, length)] = made

            over_rows(body)

            def blank(n, carry):
                target[pl.ds(pl.multiple_of(zeros[n], 32), HALO)] = jnp.zeros((HALO, 256), bf16)
                return carry

            if index < 3:
                lax.fori_loop(0, blanks, blank, 0)

        layer(0, x_stack, h_a, first_weight[...])
        layer(1, h_a, h_b, deep_weight[0])
        layer(2, h_b, h_a, deep_weight[1])
        layer(3, h_a, h_b, deep_weight[2])

        def gather(n, carry):
            for u in range(4):
                index = begin + 4 * n + u
                there = index < end
                index = jnp.where(there, index, begin)
                rows = pl.multiple_of(unit[0, index] - shift + HALO, 32)
                target = pl.ds(pl.multiple_of(unit[1, index], SEG), SEG)
                weight = padded[pl.ds(jnp.where(there, unit[2, index], 0), 1)]
                made = lax.dot_general(
                    head_turned[...], h_b[pl.ds(rows, SEG)], (((1,), (1,)), ((), ())), preferred_element_type=f32
                )
                total[:, target] += made * weight
            return carry

        lax.fori_loop(0, (end - begin + 3) // 4, gather, 0)

    lax.fori_loop(0, (units + BATCH - 1) // BATCH, batch, 0)

    bias = jnp.broadcast_to(head_bias[...], (8, 128)).T[:, :1]

    scale = 1.0 / jnp.maximum(weights[...], 1.0)
    for k in range(NSEG):
        made = total[:, k * SEG : (k + 1) * SEG] + bias * weights[k : k + 1]
        sums[pl.ds(k * SEG, SEG)] = (made * scale[k : k + 1]).astype(bf16).T
        lent = total[:, SHARD + k * SEG : SHARD + (k + 1) * SEG] * scale[NSEG + k : NSEG + k + 1]
        lent_sums[pl.ds(k * SEG, SEG)] = lent.astype(bf16).T


def run_network(count, table, shares, feats, lent, norms, lent_norms, net, profiles):
    vmem, smem, hbm = (pl.BlockSpec(memory_space=m) for m in (pltpu.VMEM, pltpu.SMEM, pl.ANY))
    first_weight, deep_weight, layer_bias, head_weight, head_bias = net
    return pl.pallas_call(
        functools.partial(network_kernel, count),
        out_shape=[
            jax.ShapeDtypeStruct((SHARD, 128), bf16),
            jax.ShapeDtypeStruct((SHARD, 128), bf16),
        ],
        in_specs=[smem, smem, hbm, hbm, hbm, hbm, hbm, hbm, vmem, hbm, vmem, vmem],
        out_specs=[vmem, vmem],
        scratch_shapes=[
            pltpu.VMEM((SHARD + HALO + 4 * (512 + HALO), 128), bf16),
            pltpu.VMEM((10 * SLOTS, 128), f32),
            pltpu.VMEM((384, 256), bf16),
            pltpu.VMEM((3, 768, 256), bf16),
            pltpu.VMEM((256, 128), bf16),
            pltpu.VMEM((CAPACITY + HALO, 128), bf16),
            pltpu.VMEM((CAPACITY + HALO, 256), bf16),
            pltpu.VMEM((CAPACITY + HALO, 256), bf16),
            pltpu.VMEM((128, 2 * SHARD), f32),
            pltpu.VMEM((128, 256), bf16),
            pltpu.VMEM((4 * 32, SEG), f32),
            pltpu.VMEM((2 * NSEG, SEG), f32),
            pltpu.SMEM((6, UNITS), i32),
            pltpu.SMEM((BATCH,), i32),
            pltpu.SemaphoreType.DMA((13,)),
        ],
        compiler_params=pltpu.CompilerParams(vmem_limit_bytes=62 * 2**20),
    )(table, shares, feats, lent, norms, lent_norms, first_weight, deep_weight, layer_bias, head_weight, head_bias, profiles)


def return_kernel(lent_sums, arrived, send_sem, recv_sem):
    me = lax.axis_index("tm")
    place = coordinates(me)
    barrier = pltpu.get_barrier_semaphore()
    for k in range(4):
        for partner in (helper(place, k), helped(place, k)):
            pl.semaphore_signal(barrier, inc=1, device_id=(partner,), device_id_type=MESH)
    pl.semaphore_wait(barrier, 8)
    copies = []
    for k in range(4):
        rows = pl.ds(512 * k, 512)
        copy = pltpu.make_async_remote_copy(
            src_ref=lent_sums.at[rows], dst_ref=arrived.at[rows], send_sem=send_sem.at[k], recv_sem=recv_sem.at[k],
            device_id=(helped(place, k),), device_id_type=MESH,
        )
        copy.start()
        copies.append(copy)
    for copy in copies:
        copy.wait()


def bring_back(lent_sums):
    hbm = pl.BlockSpec(memory_space=pl.ANY)
    return pl.pallas_call(
        return_kernel,
        out_shape=jax.ShapeDtypeStruct((SHARD, 128), bf16),
        in_specs=[hbm],
        out_specs=hbm,
        scratch_shapes=[pltpu.SemaphoreType.DMA((4,)), pltpu.SemaphoreType.DMA((4,))],
        compiler_params=pltpu.CompilerParams(
            collective_id=1, has_side_effects=True, vmem_limit_bytes=56 * 2**20
        ),
    )(lent_sums)


def per_device(
    stream, stem_weight, stem_bias, first_weight, deep_weight, layer_bias, head_weight, head_bias,
    profiles, starts, profile_index, counts,
):
    count = lax.axis_size("tm")
    feats, norms, table, shares, lent, lent_norms = make_features(
        count, starts, profile_index, counts, stream, stem_weight.reshape(7 * 128, 128), stem_bias.reshape(1, 128)
    )
    net = (
        first_weight.reshape(3 * 128, 256),
        deep_weight.reshape(3, 3 * 256, 256),
        layer_bias,
        head_weight,
        head_bias.reshape(1, 128),
    )
    sums, lent_sums = run_network(count, table, shares, feats, lent, norms, lent_norms, net, profiles)
    return (sums.astype(f32) + bring_back(lent_sums).astype(f32)).astype(bf16)


def solution(mesh):
    in_specs = (P("tm", None), P(), P(), P(), P(), P(), P(), P(), P(), P("tm"), P("tm"), P("tm"))
    return jax.shard_map(
        per_device, mesh=mesh, in_specs=in_specs, out_specs=P("tm", None), check_vma=False
    )
```

```python
import functools
import math

import jax
import jax.numpy as jnp
from jax import lax
from jax.experimental import pallas as pl
from jax.experimental.pallas import tpu as pltpu
from jax.sharding import PartitionSpec as P

bf16, f32, i32 = jnp.bfloat16, jnp.float32, jnp.int32
MESH = pl.DeviceIdType.MESH
EPS = 1e-05
SEG = 256
HALO = 32
WSEG = 16
SWEEPS = 3
SHARD = 2048
NSEG = SHARD // SEG
SLOTS = 16
TAIL = 48
EDGE = TAIL + HALO
DEAD = -100000
G1 = math.sqrt(2.0 / math.pi)
G2 = G1 * 0.044715


def gelu32(v):
    half = 0.5 * v
    return half + half * jnp.tanh(v * (G1 + G2 * (v * v)))


def gelu16(v):
    v = v.astype(bf16)
    half = bf16(0.5) * v
    return half + half * jnp.tanh(v * (bf16(G1) + bf16(G2) * (v * v)))


def coordinates(d):
    return lax.div(d, 32), lax.rem(lax.div(d, 8), 4), lax.rem(lax.div(d, 2), 4), lax.rem(d, 2)


def device_at(y, z, x, core):
    return y * 32 + z * 8 + x * 2 + core


def helper(place, k):
    y, z, x, core = place
    if k == 0:
        return device_at(lax.rem(y + 1, 4), z, x, 1 - core)
    if k == 1:
        return device_at(lax.rem(y + 3, 4), z, x, core)
    if k == 2:
        return device_at(y, lax.rem(z + 1, 4), x, 1 - core)
    return device_at(y, lax.rem(z + 3, 4), x, core)


def helped(place, k):
    y, z, x, core = place
    if k == 0:
        return device_at(lax.rem(y + 3, 4), z, x, 1 - core)
    if k == 1:
        return device_at(lax.rem(y + 1, 4), z, x, core)
    if k == 2:
        return device_at(y, lax.rem(z + 3, 4), x, 1 - core)
    return device_at(y, lax.rem(z + 1, 4), x, core)


def lanes_core(v, lane):
    return jnp.where(lane % 2 == 0, pltpu.roll(v, 127, 1), pltpu.roll(v, 1, 1))


def lanes_y(v, lane, step):
    return pltpu.roll(v, 96 if step > 0 else 32, 1)


def lanes_z(v, lane, step):
    if step > 0:
        return jnp.where(lane % 32 < 24, pltpu.roll(v, 120, 1), pltpu.roll(v, 24, 1))
    return jnp.where(lane % 32 >= 8, pltpu.roll(v, 8, 1), pltpu.roll(v, 104, 1))


def at_helper(v, lane, k):
    if k == 0:
        return lanes_y(lanes_core(v, lane), lane, 1)
    if k == 1:
        return lanes_y(v, lane, -1)
    if k == 2:
        return lanes_z(lanes_core(v, lane), lane, 1)
    return lanes_z(v, lane, -1)


def at_helped(v, lane, k):
    if k == 0:
        return lanes_core(lanes_y(v, lane, -1), lane)
    if k == 1:
        return lanes_y(v, lane, 1)
    if k == 2:
        return lanes_core(lanes_z(v, lane, -1), lane)
    return lanes_z(v, lane, 1)


def share_out(rows):
    lane = lax.broadcasted_iota(i32, (8, 128), 1)
    segment = (lane * NSEG + lax.broadcasted_iota(i32, (8, 128), 0)).astype(f32)
    covering = jnp.zeros((8, 128), f32)
    for j in range(4):
        start = jnp.broadcast_to(rows[j : j + 1], (8, 128))
        for offset in range(-2, 2):
            moved = pltpu.roll(start, (-offset) % 128, 1) if offset else start
            there = jnp.logical_and(lane + offset >= 0, lane + offset < 128)
            there = jnp.logical_and(there, jnp.logical_and(segment >= moved, segment < moved + WSEG))
            covering = covering + jnp.where(there, 1.0, 0.0)
    caps = [
        jnp.broadcast_to(covering[2 * k : 2 * k + 1] + covering[2 * k + 1 : 2 * k + 2], (8, 128))
        for k in range(4)
    ]
    load = caps[0] + caps[1] + caps[2] + caps[3]
    given = [jnp.zeros((8, 128), f32) for _ in range(4)]
    for _ in range(SWEEPS):
        for k in range(4):
            half = 0.5 * (load - at_helper(load, lane, k))
            move = jnp.where(half >= 0, jnp.floor(half), -jnp.floor(-half))
            move = jnp.clip(move, -given[k], caps[k] - given[k])
            given[k] = given[k] + move
            load = load - move + at_helped(move, lane, k)
    return given


def feature_kernel(
    count, starts, profile_index, live, stream, weight_hbm, bias, feats, norms, table, shares, lent, lent_norms,
    rows, weight, stats, mine, known, nearby, edge, local_sem, edge_send, edge_recv, line_send, line_recv, stat_send,
    stat_recv, known_send, known_recv,
    lent_send, lent_recv, norm_send, norm_recv,
):
    me = lax.axis_index("tm")
    place = coordinates(me)

    def at(offset):
        return lax.rem(me + offset + count, count)

    loads = [
        pltpu.make_async_copy(src, dst, local_sem.at[n])
        for n, (src, dst) in enumerate(
            (
                (stream, rows.at[pl.ds(TAIL, SHARD)]),
                (weight_hbm, weight),
                (stream.at[pl.ds(SHARD - TAIL, TAIL)], edge.at[pl.ds(2 * EDGE, TAIL)]),
                (stream.at[pl.ds(0, HALO)], edge.at[pl.ds(EDGE + TAIL, HALO)]),
            )
        )
    ]
    for copy in loads:
        copy.start()

    lane = lax.broadcasted_iota(i32, (1, 128), 1)
    line = jnp.zeros((1, 128), f32)
    for j in range(4):
        start = jnp.where(j < live[0], starts[j] // SEG, DEAD).astype(f32)
        line = jnp.where(lane == j, start, line)
        line = jnp.where(lane == 4 + j, profile_index[j].astype(f32), line)
    known[me] = line
    nearby[2] = line

    barrier = pltpu.get_barrier_semaphore()
    partners = [at(offset) for offset in (-2, -1, 1, 2)]
    partners += [lax.div(me, 8) * 8 + lax.rem(me + step, 8) for step in range(1, 8)]
    partners += [lax.rem(me + 8 * step, count) for step in range(1, 16)]
    for k in range(4):
        partners += [helper(place, k), helped(place, k)]
    for partner in partners:
        pl.semaphore_signal(barrier, inc=1, device_id=(partner,), device_id_type=MESH)

    def send(src, dst, send_sem, recv_sem, device):
        copy = pltpu.make_async_remote_copy(
            src_ref=src, dst_ref=dst, send_sem=send_sem, recv_sem=recv_sem, device_id=(device,),
            device_id_type=MESH,
        )
        copy.start()
        return copy

    def tell(first, length, index, device):
        block = known.at[pl.ds(first, length)]
        return send(block, block, known_send.at[index], known_recv.at[index], device)

    def convolved(block, length):
        wide = jnp.concatenate([block[13 + k : 13 + k + length] for k in range(7)], axis=1)
        return gelu32(jnp.dot(wide, weight[...], preferred_element_type=f32) + bias[...])

    def stem(first, length):
        block = rows[pl.ds(first + 32, length + 32)]
        feats[pl.ds(first + HALO, length)] = convolved(block, length).astype(bf16)

    def lend(k):
        return send(
            feats.at[pl.ds(512 * k, 512 + HALO)], lent.at[k], lent_send.at[k], lent_recv.at[k], helper(place, k)
        )

    pl.semaphore_wait(barrier, len(partners))
    edges = [
        send(
            stream.at[pl.ds(SHARD - TAIL, TAIL)], edge.at[pl.ds((2 - offset) * EDGE, TAIL)],
            edge_send.at[index], edge_recv.at[index], at(offset),
        )
        for index, offset in enumerate((2, 1, -1))
    ] + [
        send(
            stream.at[pl.ds(0, HALO)], edge.at[pl.ds((1 - offset) * EDGE + TAIL, HALO)],
            edge_send.at[3 + index], edge_recv.at[3 + index], at(offset),
        )
        for index, offset in enumerate((1, -1, -2))
    ]
    lines = [
        send(known.at[me], nearby.at[2 - offset], line_send.at[index], line_recv.at[index], at(offset))
        for index, offset in enumerate((2, 1, -1))
    ]
    eight = lax.div(me, 8) * 8
    near = [tell(me, 1, step - 1, eight + lax.rem(me + step, 8)) for step in range(1, 8)]
    for copy in loads:
        copy.wait()
    stem(16, 496)
    stem(512, 512)
    stem(1024, 512)
    stem(1536, 496)
    for k in range(NSEG):
        low, high = max(k * SEG, 16), min(k * SEG + SEG, SHARD - 16)
        part = feats[pl.ds(low + HALO, high - low)].astype(f32)
        for n, total in enumerate((part, part * part)):
            total = jnp.sum(total, axis=0, keepdims=True)
            mine[n, k : k + 1] = total
            stats[n, 16 + k : 17 + k] = total
    moments = [
        send(mine, stats.at[:, pl.ds(8 * (2 - offset), 8)], stat_send.at[index], stat_recv.at[index], at(offset))
        for index, offset in enumerate((-2, -1, 1, 2))
    ]
    for copy in near:
        copy.wait()
    far = [tell(eight, 8, 6 + step, lax.rem(me + 8 * step, count)) for step in range(1, 16)]
    for copy in edges:
        copy.wait()
    for b in range(4):

        @pl.when(me - 2 + b == -1)
        def _():
            edge[pl.ds(b * EDGE, TAIL)] = jnp.zeros((TAIL, 128), bf16)

        @pl.when(me - 2 + b == count - 1)
        def _():
            edge[pl.ds(b * EDGE + TAIL, HALO)] = jnp.zeros((HALO, 128), bf16)

    rows[pl.ds(0, TAIL)] = edge[pl.ds(EDGE, TAIL)]
    rows[pl.ds(SHARD + TAIL, 16)] = edge[pl.ds(2 * EDGE + TAIL, 16)]
    stem(-HALO, HALO + 16)
    stem(SHARD - 16, 16)
    loans = [lend(k) for k in range(4)]
    ends = convolved(edge[...], 4 * EDGE - 32).astype(bf16).astype(f32)
    for copy in moments + lines:
        copy.wait()
    for b in range(4):
        for side in range(2):
            part = ends[b * EDGE + 16 * (1 + side) : b * EDGE + 16 * (2 + side)]
            row = 8 * b + 7 + side
            stats[0, row : row + 1] += jnp.sum(part, axis=0, keepdims=True)
            stats[1, row : row + 1] += jnp.sum(part * part, axis=0, keepdims=True)

    row = lax.broadcasted_iota(i32, (40, 128), 0).astype(f32)
    for slot in range(SLOTS):
        start = nearby[slot // 4][:, slot % 4 : slot % 4 + 1]
        first = start - (NSEG * me - 16).astype(f32)
        covered = jnp.logical_and(row >= first, row < first + WSEG)
        mean, square = (
            jnp.sum(jnp.where(covered, stats[n], 0.0), axis=0, keepdims=True) * (1.0 / (WSEG * SEG))
            for n in range(2)
        )
        scale = lax.rsqrt(square - mean * mean + EPS)
        norms[slot : slot + 1] = scale
        norms[SLOTS + slot : SLOTS + slot + 1] = -mean * scale
    for k in range(4):
        loans.append(send(norms, lent_norms.at[k], norm_send.at[k], norm_recv.at[k], helper(place, k)))

    for copy in far:
        copy.wait()
    turned = known[...].reshape(128, 128).T[:8]
    table[...] = turned.astype(i32)
    given = share_out(turned)
    shares[...] = jnp.concatenate([given[k][:1] for k in range(4)] + [jnp.zeros((4, 128), f32)], axis=0).astype(i32)
    for copy in loans:
        copy.wait()


def make_features(count, starts, profile_index, counts, stream, weight, bias):
    vmem, smem, hbm = (pl.BlockSpec(memory_space=m) for m in (pltpu.VMEM, pltpu.SMEM, pl.ANY))
    dma = pltpu.SemaphoreType.DMA
    return pl.pallas_call(
        functools.partial(feature_kernel, count),
        out_shape=[
            jax.ShapeDtypeStruct((SHARD + HALO, 128), bf16),
            jax.ShapeDtypeStruct((2 * SLOTS, 128), f32),
            jax.ShapeDtypeStruct((8, 128), i32),
            jax.ShapeDtypeStruct((8, 128), i32),
            jax.ShapeDtypeStruct((4, 512 + HALO, 128), bf16),
            jax.ShapeDtypeStruct((4, 2 * SLOTS, 128), f32),
        ],
        in_specs=[smem, smem, smem, hbm, hbm, vmem],
        out_specs=[vmem, vmem, vmem, vmem, hbm, hbm],
        scratch_shapes=[
            pltpu.VMEM((SHARD + 64, 128), bf16),
            pltpu.VMEM((7 * 128, 128), bf16),
            pltpu.VMEM((2, 40, 128), f32),
            pltpu.VMEM((2, NSEG, 128), f32),
            pltpu.VMEM((128, 1, 128), f32),
            pltpu.VMEM((5, 1, 128), f32),
            pltpu.VMEM((4 * EDGE, 128), bf16),
            dma((4,)),
            dma((6,)), dma((6,)),
            dma((3,)), dma((3,)),
            dma((4,)), dma((4,)),
            dma((22,)), dma((22,)),
            dma((4,)), dma((4,)),
            dma((4,)), dma((4,)),
        ],
        compiler_params=pltpu.CompilerParams(
            collective_id=0, has_side_effects=True, vmem_limit_bytes=56 * 2**20
        ),
    )(starts, profile_index, counts, stream, weight, bias)


SIZES = (4608, 2304, 1152, 576)
BATCH = 48
CAPACITY = -(-BATCH * (SEG + HALO) // SIZES[-1]) * SIZES[-1]
UNITS = 136
TOGETHER = 6


def network_kernel(
    count, table, shares, feats_hbm, lent_hbm, norms_hbm, lent_norms_hbm, first_hbm, deep_hbm, layer_bias, head_hbm,
    head_bias, profiles, sums, lent_sums, feats, norms, first_weight, deep_weight, head_weight, x_stack, h_a,
    h_b, total, head_turned, padded, weights, unit, zeros, sems,
):
    me = lax.axis_index("tm")
    place = coordinates(me)
    pieces = [
        (first_hbm, first_weight),
        (deep_hbm, deep_weight),
        (head_hbm, head_weight),
        (feats_hbm, feats.at[pl.ds(0, SHARD + HALO)]),
        (norms_hbm, norms.at[pl.ds(0, 2 * SLOTS)]),
    ]
    for k in range(4):
        pieces.append((lent_hbm.at[k], feats.at[pl.ds(SHARD + HALO + (512 + HALO) * k, 512 + HALO)]))
        pieces.append((lent_norms_hbm.at[k], norms.at[pl.ds(2 * SLOTS * (k + 1), 2 * SLOTS)]))
    loads = [pltpu.make_async_copy(src, dst, sems.at[n]) for n, (src, dst) in enumerate(pieces)]
    for copy in loads[3:] + loads[:3]:
        copy.start()

    padded[...] = jnp.zeros_like(padded)
    for p in range(4):
        for k in range(WSEG):
            padded[p * 32 + 8 + k : p * 32 + 9 + k] = profiles[p : p + 1, k * SEG : (k + 1) * SEG]
    weights[...] = jnp.zeros_like(weights)

    def clear(index, carry):
        total[:, pl.ds(pl.multiple_of(index * SEG, SEG), SEG)] = jnp.zeros((128, SEG), f32)
        return carry

    lax.fori_loop(0, 2 * NSEG, clear, 0)

    def window(home, slot):
        owner = home + slot // 4 - 2
        inside = jnp.logical_and(owner >= 0, owner < count)
        owner = jnp.clip(owner, 0, count - 1)
        start = jnp.where(inside, table[lax.rem(slot, 4), owner], DEAD)
        return start - NSEG * home, table[4 + lax.rem(slot, 4), owner]

    def put(base, target, norm, rel, profile, low, high, fresh, state):
        def segment(k, state):
            rows, units = state
            ahead = jnp.where(jnp.logical_and(k == low, fresh), jnp.where(k == rel, 2, 1), 0)
            rows = rows + jnp.where(ahead > 0, HALO, 0)
            unit[0, units] = rows
            unit[1, units] = target + k * SEG
            unit[2, units] = profile * 32 + 8 + k - rel
            unit[3, units] = base + k * SEG
            unit[4, units] = norm
            unit[5, units] = ahead
            return rows + SEG, units + 1

        return lax.fori_loop(low, high, segment, state)

    def own_slot(slot, carry):
        rel, profile = window(me, slot)

        def covered(carry):
            for k in range(NSEG):
                weights[k : k + 1] += padded[pl.ds(profile * 32 + 8 - rel + k, 1)]
            state, lefts = carry[:2], list(carry[2:])
            end = i32(-1)
            for k in range(4):
                first = jnp.maximum(rel, 2 * k)
                high = jnp.minimum(rel + WSEG, 2 * k + 2)
                given = jnp.minimum(lefts[k], jnp.maximum(high - first, 0))
                lefts[k] = lefts[k] - given
                low = first + given
                state = put(0, 0, slot, rel, profile, low, high, low != end, state)
                end = jnp.where(high > low, high, end)
            return (*state, *lefts)

        return lax.cond(jnp.logical_and(rel > -WSEG, rel < NSEG), covered, lambda c: c, carry)

    carry = lax.fori_loop(0, SLOTS, own_slot, (i32(0), i32(0), *(shares[k, me] for k in range(4))))
    state = carry[:2]
    for k in range(4):
        home = helped(place, k)
        share = shares[k, home]

        def lent_slot(slot, carry, k=k, home=home):
            rel, profile = window(home, slot)

            def covered(carry):
                for i in range(2):
                    row = NSEG + 2 * k + i
                    weights[row : row + 1] += padded[pl.ds(profile * 32 + 8 - rel + 2 * k + i, 1)]
                first = jnp.maximum(rel, 2 * k)
                taken = jnp.minimum(carry[2], jnp.maximum(jnp.minimum(rel + WSEG, 2 * k + 2) - first, 0))
                state = put(
                    SHARD + HALO + HALO * k, SHARD, SLOTS * (k + 1) + slot, rel, profile, first, first + taken,
                    True, carry[:2],
                )
                return (*state, carry[2] - taken)

            return lax.cond(jnp.logical_and(rel > -WSEG, rel < NSEG), covered, lambda c: c, carry)

        state = lax.fori_loop(0, jnp.where(share > 0, SLOTS, 0), lent_slot, (*state, share))[:2]
    rows, units = state
    unit[0, units] = rows + HALO

    for copy in loads:
        copy.wait()
    for half in range(2):
        part = head_weight[pl.ds(half * 128, 128)].astype(f32)
        head_turned[:, half * 128 : (half + 1) * 128] = part.T.astype(bf16)

    def batch(b, carry):
        begin, end = b * BATCH, jnp.minimum(b * BATCH + BATCH, units)
        shift = unit[0, begin] - HALO

        def fill(n, blanks):
            first = pl.multiple_of(unit[0, n] - shift, 32)
            norm, source = unit[4, n], pl.multiple_of(unit[3, n], 32)
            scale = norms[pl.ds(norm // SLOTS * 2 * SLOTS + norm % SLOTS, 1)]
            offset = norms[pl.ds(norm // SLOTS * 2 * SLOTS + SLOTS + norm % SLOTS, 1)]
            ahead = jnp.where(jnp.logical_and(n == begin, unit[5, n] == 0), 1, unit[5, n])

            def normalised(row, length):
                return (feats[pl.ds(row, length)].astype(f32) * scale + offset).astype(bf16)

            x_stack[pl.ds(first + HALO, SEG)] = normalised(pl.multiple_of(source + HALO, 32), SEG)

            @pl.when(ahead == 1)
            def _():
                x_stack[pl.ds(first, HALO)] = normalised(source, HALO)

            @pl.when(ahead == 2)
            def _():
                x_stack[pl.ds(first, HALO)] = jnp.zeros((HALO, 128), bf16)
                zeros[blanks] = first

            return blanks + jnp.where(ahead == 2, 1, 0)

        blanks = lax.fori_loop(begin, end, fill, i32(0))
        rows = unit[0, end - 1] - shift + SEG
        spans, first = [], i32(0)
        for size in SIZES:
            steps = (rows - first + (size - 1 if size == SIZES[-1] else 0)) // size
            spans.append((size, first, steps))
            first = first + steps * size
        run_batch(begin, end, shift, spans, blanks)
        return carry

    def run_batch(begin, end, shift, spans, blanks):
        def over_rows(body):
            for size, first, steps in spans:

                def step(index, carry, size=size, first=first):
                    body(pl.multiple_of(first + index * size, SIZES[-1]), size)
                    return carry

                lax.fori_loop(0, steps, step, 0)

        def layer(index, source, target, weight):
            spread = 2**index

            def body(first, length):
                block = source[pl.ds(first, length + HALO)]
                width, summed = block.shape[1], layer_bias[index : index + 1]
                shifted = [block[HALO - s * spread : HALO - s * spread + length] for s in (2, 1, 0)]
                if index == 0:
                    shifted = [jnp.concatenate(shifted[:2], axis=1), shifted[2]]
                start = 0
                for rows_of in shifted:
                    part = weight[start : start + rows_of.shape[1]]
                    start = start + rows_of.shape[1]
                    summed = summed + jnp.dot(rows_of, part, preferred_element_type=f32)
                made = gelu16(summed)
                if index:
                    made = made + block[HALO:]
                target[pl.ds(first + HALO, length)] = made

            over_rows(body)

            def blank(n, carry):
                target[pl.ds(pl.multiple_of(zeros[n], 32), HALO)] = jnp.zeros((HALO, 256), bf16)
                return carry

            if index < 3:
                lax.fori_loop(0, blanks, blank, 0)

        layer(0, x_stack, h_a, first_weight[...])
        layer(1, h_a, h_b, deep_weight[0])
        layer(2, h_b, h_a, deep_weight[1])
        layer(3, h_a, h_b, deep_weight[2])

        def gather(n, carry):
            for u in range(TOGETHER):
                index = begin + TOGETHER * n + u
                there = index < end
                index = jnp.where(there, index, begin)
                rows = pl.multiple_of(unit[0, index] - shift + HALO, 32)
                target = pl.ds(pl.multiple_of(unit[1, index], SEG), SEG)
                weight = padded[pl.ds(jnp.where(there, unit[2, index], 0), 1)]
                made = lax.dot_general(
                    head_turned[...], h_b[pl.ds(rows, SEG)], (((1,), (1,)), ((), ())), preferred_element_type=f32
                )
                total[:, target] += made * weight
            return carry

        lax.fori_loop(0, (end - begin + TOGETHER - 1) // TOGETHER, gather, 0)

    lax.fori_loop(0, (units + BATCH - 1) // BATCH, batch, 0)

    bias = jnp.broadcast_to(head_bias[...], (8, 128)).T[:, :1]

    scale = 1.0 / jnp.maximum(weights[...], 1.0)
    for k in range(NSEG):
        made = total[:, k * SEG : (k + 1) * SEG] + bias * weights[k : k + 1]
        sums[pl.ds(k * SEG, SEG)] = (made * scale[k : k + 1]).astype(bf16).T
        lent = total[:, SHARD + k * SEG : SHARD + (k + 1) * SEG] * scale[NSEG + k : NSEG + k + 1]
        lent_sums[pl.ds(k * SEG, SEG)] = lent.astype(bf16).T


def run_network(count, table, shares, feats, lent, norms, lent_norms, net, profiles):
    vmem, smem, hbm = (pl.BlockSpec(memory_space=m) for m in (pltpu.VMEM, pltpu.SMEM, pl.ANY))
    first_weight, deep_weight, layer_bias, head_weight, head_bias = net
    return pl.pallas_call(
        functools.partial(network_kernel, count),
        out_shape=[
            jax.ShapeDtypeStruct((SHARD, 128), bf16),
            jax.ShapeDtypeStruct((SHARD, 128), bf16),
        ],
        in_specs=[smem, smem, hbm, hbm, hbm, hbm, hbm, hbm, vmem, hbm, vmem, vmem],
        out_specs=[vmem, vmem],
        scratch_shapes=[
            pltpu.VMEM((SHARD + HALO + 4 * (512 + HALO), 128), bf16),
            pltpu.VMEM((10 * SLOTS, 128), f32),
            pltpu.VMEM((384, 256), bf16),
            pltpu.VMEM((3, 768, 256), bf16),
            pltpu.VMEM((256, 128), bf16),
            pltpu.VMEM((CAPACITY + HALO, 128), bf16),
            pltpu.VMEM((CAPACITY + HALO, 256), bf16),
            pltpu.VMEM((CAPACITY + HALO, 256), bf16),
            pltpu.VMEM((128, 2 * SHARD), f32),
            pltpu.VMEM((128, 256), bf16),
            pltpu.VMEM((4 * 32, SEG), f32),
            pltpu.VMEM((2 * NSEG, SEG), f32),
            pltpu.SMEM((6, UNITS), i32),
            pltpu.SMEM((BATCH,), i32),
            pltpu.SemaphoreType.DMA((13,)),
        ],
        compiler_params=pltpu.CompilerParams(vmem_limit_bytes=62 * 2**20),
    )(table, shares, feats, lent, norms, lent_norms, first_weight, deep_weight, layer_bias, head_weight, head_bias, profiles)


def return_kernel(lent_sums, arrived, send_sem, recv_sem):
    me = lax.axis_index("tm")
    place = coordinates(me)
    barrier = pltpu.get_barrier_semaphore()
    for k in range(4):
        for partner in (helper(place, k), helped(place, k)):
            pl.semaphore_signal(barrier, inc=1, device_id=(partner,), device_id_type=MESH)
    pl.semaphore_wait(barrier, 8)
    copies = []
    for k in range(4):
        rows = pl.ds(512 * k, 512)
        copy = pltpu.make_async_remote_copy(
            src_ref=lent_sums.at[rows], dst_ref=arrived.at[rows], send_sem=send_sem.at[k], recv_sem=recv_sem.at[k],
            device_id=(helped(place, k),), device_id_type=MESH,
        )
        copy.start()
        copies.append(copy)
    for copy in copies:
        copy.wait()


def bring_back(lent_sums):
    hbm = pl.BlockSpec(memory_space=pl.ANY)
    return pl.pallas_call(
        return_kernel,
        out_shape=jax.ShapeDtypeStruct((SHARD, 128), bf16),
        in_specs=[hbm],
        out_specs=hbm,
        scratch_shapes=[pltpu.SemaphoreType.DMA((4,)), pltpu.SemaphoreType.DMA((4,))],
        compiler_params=pltpu.CompilerParams(
            collective_id=1, has_side_effects=True, vmem_limit_bytes=56 * 2**20
        ),
    )(lent_sums)


def per_device(
    stream, stem_weight, stem_bias, first_weight, deep_weight, layer_bias, head_weight, head_bias,
    profiles, starts, profile_index, counts,
):
    count = lax.axis_size("tm")
    feats, norms, table, shares, lent, lent_norms = make_features(
        count, starts, profile_index, counts, stream, stem_weight.reshape(7 * 128, 128), stem_bias.reshape(1, 128)
    )
    net = (
        first_weight.reshape(3 * 128, 256),
        deep_weight.reshape(3, 3 * 256, 256),
        layer_bias,
        head_weight,
        head_bias.reshape(1, 128),
    )
    sums, lent_sums = run_network(count, table, shares, feats, lent, norms, lent_norms, net, profiles)
    return (sums.astype(f32) + bring_back(lent_sums).astype(f32)).astype(bf16)


def solution(mesh):
    in_specs = (P("tm", None), P(), P(), P(), P(), P(), P(), P(), P(), P("tm"), P("tm"), P("tm"))
    return jax.shard_map(
        per_device, mesh=mesh, in_specs=in_specs, out_specs=P("tm", None), check_vma=False
    )
```

```python
import functools
import math

import jax
import jax.numpy as jnp
from jax import lax
from jax.experimental import pallas as pl
from jax.experimental.pallas import tpu as pltpu
from jax.sharding import PartitionSpec as P

bf16, f32, i32 = jnp.bfloat16, jnp.float32, jnp.int32
MESH = pl.DeviceIdType.MESH
EPS = 1e-05
SEG = 256
HALO = 32
WSEG = 16
SWEEPS = 3
SHARD = 2048
NSEG = SHARD // SEG
SLOTS = 16
TAIL = 48
EDGE = TAIL + HALO
DEAD = -100000
G1 = math.sqrt(2.0 / math.pi)
G2 = G1 * 0.044715


def gelu32(v):
    half = 0.5 * v
    return half + half * jnp.tanh(v * (G1 + G2 * (v * v)))


def gelu16(v):
    v = v.astype(bf16)
    half = bf16(0.5) * v
    return half + half * jnp.tanh(v * (bf16(G1) + bf16(G2) * (v * v)))


def coordinates(d):
    return lax.div(d, 32), lax.rem(lax.div(d, 8), 4), lax.rem(lax.div(d, 2), 4), lax.rem(d, 2)


def device_at(y, z, x, core):
    return y * 32 + z * 8 + x * 2 + core


def helper(place, k):
    y, z, x, core = place
    if k == 0:
        return device_at(lax.rem(y + 1, 4), z, x, 1 - core)
    if k == 1:
        return device_at(lax.rem(y + 3, 4), z, x, core)
    if k == 2:
        return device_at(y, lax.rem(z + 1, 4), x, 1 - core)
    return device_at(y, lax.rem(z + 3, 4), x, core)


def helped(place, k):
    y, z, x, core = place
    if k == 0:
        return device_at(lax.rem(y + 3, 4), z, x, 1 - core)
    if k == 1:
        return device_at(lax.rem(y + 1, 4), z, x, core)
    if k == 2:
        return device_at(y, lax.rem(z + 3, 4), x, 1 - core)
    return device_at(y, lax.rem(z + 1, 4), x, core)


def lanes_core(v, lane):
    return jnp.where(lane % 2 == 0, pltpu.roll(v, 127, 1), pltpu.roll(v, 1, 1))


def lanes_y(v, lane, step):
    return pltpu.roll(v, 96 if step > 0 else 32, 1)


def lanes_z(v, lane, step):
    if step > 0:
        return jnp.where(lane % 32 < 24, pltpu.roll(v, 120, 1), pltpu.roll(v, 24, 1))
    return jnp.where(lane % 32 >= 8, pltpu.roll(v, 8, 1), pltpu.roll(v, 104, 1))


def at_helper(v, lane, k):
    if k == 0:
        return lanes_y(lanes_core(v, lane), lane, 1)
    if k == 1:
        return lanes_y(v, lane, -1)
    if k == 2:
        return lanes_z(lanes_core(v, lane), lane, 1)
    return lanes_z(v, lane, -1)


def at_helped(v, lane, k):
    if k == 0:
        return lanes_core(lanes_y(v, lane, -1), lane)
    if k == 1:
        return lanes_y(v, lane, 1)
    if k == 2:
        return lanes_core(lanes_z(v, lane, -1), lane)
    return lanes_z(v, lane, 1)


def share_out(rows):
    lane = lax.broadcasted_iota(i32, (8, 128), 1)
    segment = (lane * NSEG + lax.broadcasted_iota(i32, (8, 128), 0)).astype(f32)
    covering = jnp.zeros((8, 128), f32)
    for j in range(4):
        start = jnp.broadcast_to(rows[j : j + 1], (8, 128))
        for offset in range(-2, 2):
            moved = pltpu.roll(start, (-offset) % 128, 1) if offset else start
            there = jnp.logical_and(lane + offset >= 0, lane + offset < 128)
            there = jnp.logical_and(there, jnp.logical_and(segment >= moved, segment < moved + WSEG))
            covering = covering + jnp.where(there, 1.0, 0.0)
    caps = [
        jnp.broadcast_to(covering[2 * k : 2 * k + 1] + covering[2 * k + 1 : 2 * k + 2], (8, 128))
        for k in range(4)
    ]
    load = caps[0] + caps[1] + caps[2] + caps[3]
    given = [jnp.zeros((8, 128), f32) for _ in range(4)]
    for _ in range(SWEEPS):
        for k in range(4):
            half = 0.5 * (load - at_helper(load, lane, k))
            move = jnp.where(half >= 0, jnp.floor(half), -jnp.floor(-half))
            move = jnp.clip(move, -given[k], caps[k] - given[k])
            given[k] = given[k] + move
            load = load - move + at_helped(move, lane, k)
    return given


def feature_kernel(
    count, starts, profile_index, live, stream, weight_hbm, bias, feats, norms, table, shares, lent, lent_norms,
    rows, weight, stats, mine, known, nearby, edge, local_sem, edge_send, edge_recv, line_send, line_recv, stat_send,
    stat_recv, known_send, known_recv,
    lent_send, lent_recv, norm_send, norm_recv,
):
    me = lax.axis_index("tm")
    place = coordinates(me)

    def at(offset):
        return lax.rem(me + offset + count, count)

    loads = [
        pltpu.make_async_copy(src, dst, local_sem.at[n])
        for n, (src, dst) in enumerate(
            (
                (stream, rows.at[pl.ds(TAIL, SHARD)]),
                (weight_hbm, weight),
                (stream.at[pl.ds(SHARD - TAIL, TAIL)], edge.at[pl.ds(2 * EDGE, TAIL)]),
                (stream.at[pl.ds(0, HALO)], edge.at[pl.ds(EDGE + TAIL, HALO)]),
            )
        )
    ]
    for copy in loads:
        copy.start()

    lane = lax.broadcasted_iota(i32, (1, 128), 1)
    line = jnp.zeros((1, 128), f32)
    for j in range(4):
        start = jnp.where(j < live[0], starts[j] // SEG, DEAD).astype(f32)
        line = jnp.where(lane == j, start, line)
        line = jnp.where(lane == 4 + j, profile_index[j].astype(f32), line)
    known[me] = line
    nearby[2] = line

    barrier = pltpu.get_barrier_semaphore()
    partners = [at(offset) for offset in (-2, -1, 1, 2)]
    partners += [lax.div(me, 8) * 8 + lax.rem(me + step, 8) for step in range(1, 8)]
    partners += [lax.rem(me + 8 * step, count) for step in range(1, 16)]
    for k in range(4):
        partners += [helper(place, k), helped(place, k)]
    for partner in partners:
        pl.semaphore_signal(barrier, inc=1, device_id=(partner,), device_id_type=MESH)

    def send(src, dst, send_sem, recv_sem, device):
        copy = pltpu.make_async_remote_copy(
            src_ref=src, dst_ref=dst, send_sem=send_sem, recv_sem=recv_sem, device_id=(device,),
            device_id_type=MESH,
        )
        copy.start()
        return copy

    def tell(first, length, index, device):
        block = known.at[pl.ds(first, length)]
        return send(block, block, known_send.at[index], known_recv.at[index], device)

    def convolved(block, length):
        wide = jnp.concatenate([block[13 + k : 13 + k + length] for k in range(7)], axis=1)
        return gelu32(jnp.dot(wide, weight[...], preferred_element_type=f32) + bias[...])

    def stem(first, length):
        block = rows[pl.ds(first + 32, length + 32)]
        feats[pl.ds(first + HALO, length)] = convolved(block, length).astype(bf16)

    def lend(k):
        return send(
            feats.at[pl.ds(512 * k, 512 + HALO)], lent.at[k], lent_send.at[k], lent_recv.at[k], helper(place, k)
        )

    pl.semaphore_wait(barrier, len(partners))
    eight = lax.div(me, 8) * 8
    near = [tell(me, 1, step - 1, eight + lax.rem(me + step, 8)) for step in range(1, 8)]
    edges = [
        send(
            stream.at[pl.ds(SHARD - TAIL, TAIL)], edge.at[pl.ds((2 - offset) * EDGE, TAIL)],
            edge_send.at[index], edge_recv.at[index], at(offset),
        )
        for index, offset in enumerate((2, 1, -1))
    ] + [
        send(
            stream.at[pl.ds(0, HALO)], edge.at[pl.ds((1 - offset) * EDGE + TAIL, HALO)],
            edge_send.at[3 + index], edge_recv.at[3 + index], at(offset),
        )
        for index, offset in enumerate((1, -1, -2))
    ]
    lines = [
        send(known.at[me], nearby.at[2 - offset], line_send.at[index], line_recv.at[index], at(offset))
        for index, offset in enumerate((2, 1, -1))
    ]
    for copy in loads:
        copy.wait()
    stem(16, 496)
    stem(512, 512)
    stem(1024, 512)
    stem(1536, 496)
    for k in range(NSEG):
        low, high = max(k * SEG, 16), min(k * SEG + SEG, SHARD - 16)
        part = feats[pl.ds(low + HALO, high - low)].astype(f32)
        for n, total in enumerate((part, part * part)):
            total = jnp.sum(total, axis=0, keepdims=True)
            mine[n, k : k + 1] = total
            stats[n, 16 + k : 17 + k] = total
    moments = [
        send(mine, stats.at[:, pl.ds(8 * (2 - offset), 8)], stat_send.at[index], stat_recv.at[index], at(offset))
        for index, offset in enumerate((-2, -1, 1, 2))
    ]
    for copy in near:
        copy.wait()
    far = [tell(eight, 8, 6 + step, lax.rem(me + 8 * step, count)) for step in range(1, 16)]
    for copy in edges:
        copy.wait()
    for b in range(4):

        @pl.when(me - 2 + b == -1)
        def _():
            edge[pl.ds(b * EDGE, TAIL)] = jnp.zeros((TAIL, 128), bf16)

        @pl.when(me - 2 + b == count - 1)
        def _():
            edge[pl.ds(b * EDGE + TAIL, HALO)] = jnp.zeros((HALO, 128), bf16)

    rows[pl.ds(0, TAIL)] = edge[pl.ds(EDGE, TAIL)]
    rows[pl.ds(SHARD + TAIL, 16)] = edge[pl.ds(2 * EDGE + TAIL, 16)]
    stem(-HALO, HALO + 16)
    stem(SHARD - 16, 16)
    loans = [lend(k) for k in range(4)]
    ends = convolved(edge[...], 4 * EDGE - 32).astype(bf16).astype(f32)
    for copy in moments + lines:
        copy.wait()
    for b in range(4):
        for side in range(2):
            part = ends[b * EDGE + 16 * (1 + side) : b * EDGE + 16 * (2 + side)]
            row = 8 * b + 7 + side
            stats[0, row : row + 1] += jnp.sum(part, axis=0, keepdims=True)
            stats[1, row : row + 1] += jnp.sum(part * part, axis=0, keepdims=True)

    row = lax.broadcasted_iota(i32, (40, 128), 0).astype(f32)
    for slot in range(SLOTS):
        start = nearby[slot // 4][:, slot % 4 : slot % 4 + 1]
        first = start - (NSEG * me - 16).astype(f32)
        covered = jnp.logical_and(row >= first, row < first + WSEG)
        mean, square = (
            jnp.sum(jnp.where(covered, stats[n], 0.0), axis=0, keepdims=True) * (1.0 / (WSEG * SEG))
            for n in range(2)
        )
        scale = lax.rsqrt(square - mean * mean + EPS)
        norms[slot : slot + 1] = scale
        norms[SLOTS + slot : SLOTS + slot + 1] = -mean * scale
    for k in range(4):
        loans.append(send(norms, lent_norms.at[k], norm_send.at[k], norm_recv.at[k], helper(place, k)))

    for copy in far:
        copy.wait()
    turned = known[...].reshape(128, 128).T[:8]
    table[...] = turned.astype(i32)
    given = share_out(turned)
    shares[...] = jnp.concatenate([given[k][:1] for k in range(4)] + [jnp.zeros((4, 128), f32)], axis=0).astype(i32)
    for copy in loans:
        copy.wait()


def make_features(count, starts, profile_index, counts, stream, weight, bias):
    vmem, smem, hbm = (pl.BlockSpec(memory_space=m) for m in (pltpu.VMEM, pltpu.SMEM, pl.ANY))
    dma = pltpu.SemaphoreType.DMA
    return pl.pallas_call(
        functools.partial(feature_kernel, count),
        out_shape=[
            jax.ShapeDtypeStruct((SHARD + HALO, 128), bf16),
            jax.ShapeDtypeStruct((2 * SLOTS, 128), f32),
            jax.ShapeDtypeStruct((8, 128), i32),
            jax.ShapeDtypeStruct((8, 128), i32),
            jax.ShapeDtypeStruct((4, 512 + HALO, 128), bf16),
            jax.ShapeDtypeStruct((4, 2 * SLOTS, 128), f32),
        ],
        in_specs=[smem, smem, smem, hbm, hbm, vmem],
        out_specs=[vmem, vmem, vmem, vmem, hbm, hbm],
        scratch_shapes=[
            pltpu.VMEM((SHARD + 64, 128), bf16),
            pltpu.VMEM((7 * 128, 128), bf16),
            pltpu.VMEM((2, 40, 128), f32),
            pltpu.VMEM((2, NSEG, 128), f32),
            pltpu.VMEM((128, 1, 128), f32),
            pltpu.VMEM((5, 1, 128), f32),
            pltpu.VMEM((4 * EDGE, 128), bf16),
            dma((4,)),
            dma((6,)), dma((6,)),
            dma((3,)), dma((3,)),
            dma((4,)), dma((4,)),
            dma((22,)), dma((22,)),
            dma((4,)), dma((4,)),
            dma((4,)), dma((4,)),
        ],
        compiler_params=pltpu.CompilerParams(
            collective_id=0, has_side_effects=True, vmem_limit_bytes=56 * 2**20
        ),
    )(starts, profile_index, counts, stream, weight, bias)


SIZES = (4608, 2304, 1152, 576, 288)
BATCH = 48
CAPACITY = -(-BATCH * (SEG + HALO) // SIZES[-1]) * SIZES[-1]
UNITS = 136
TOGETHER = 6


def network_kernel(
    count, table, shares, feats_hbm, lent_hbm, norms_hbm, lent_norms_hbm, first_hbm, deep_hbm, layer_bias, head_hbm,
    head_bias, profiles, sums, lent_sums, feats, norms, first_weight, deep_weight, head_weight, x_stack, h_a,
    h_b, total, head_turned, padded, weights, unit, zeros, sems,
):
    me = lax.axis_index("tm")
    place = coordinates(me)
    pieces = [
        (first_hbm, first_weight),
        (deep_hbm, deep_weight),
        (head_hbm, head_weight),
        (feats_hbm, feats.at[pl.ds(0, SHARD + HALO)]),
        (norms_hbm, norms.at[pl.ds(0, 2 * SLOTS)]),
    ]
    for k in range(4):
        pieces.append((lent_hbm.at[k], feats.at[pl.ds(SHARD + HALO + (512 + HALO) * k, 512 + HALO)]))
        pieces.append((lent_norms_hbm.at[k], norms.at[pl.ds(2 * SLOTS * (k + 1), 2 * SLOTS)]))
    loads = [pltpu.make_async_copy(src, dst, sems.at[n]) for n, (src, dst) in enumerate(pieces)]
    for copy in loads[3:] + loads[:3]:
        copy.start()

    padded[...] = jnp.zeros_like(padded)
    for p in range(4):
        for k in range(WSEG):
            padded[p * 32 + 8 + k : p * 32 + 9 + k] = profiles[p : p + 1, k * SEG : (k + 1) * SEG]
    weights[...] = jnp.zeros_like(weights)

    def clear(index, carry):
        total[:, pl.ds(pl.multiple_of(index * SEG, SEG), SEG)] = jnp.zeros((128, SEG), f32)
        return carry

    lax.fori_loop(0, 2 * NSEG, clear, 0)

    def window(home, slot):
        owner = home + slot // 4 - 2
        inside = jnp.logical_and(owner >= 0, owner < count)
        owner = jnp.clip(owner, 0, count - 1)
        start = jnp.where(inside, table[lax.rem(slot, 4), owner], DEAD)
        return start - NSEG * home, table[4 + lax.rem(slot, 4), owner]

    def put(base, target, norm, rel, profile, low, high, fresh, state):
        def segment(k, state):
            rows, units = state
            ahead = jnp.where(jnp.logical_and(k == low, fresh), jnp.where(k == rel, 2, 1), 0)
            rows = rows + jnp.where(ahead > 0, HALO, 0)
            unit[0, units] = rows
            unit[1, units] = target + k * SEG
            unit[2, units] = profile * 32 + 8 + k - rel
            unit[3, units] = base + k * SEG
            unit[4, units] = norm
            unit[5, units] = ahead
            return rows + SEG, units + 1

        return lax.fori_loop(low, high, segment, state)

    def own_slot(slot, carry):
        rel, profile = window(me, slot)

        def covered(carry):
            for k in range(NSEG):
                weights[k : k + 1] += padded[pl.ds(profile * 32 + 8 - rel + k, 1)]
            state, lefts = carry[:2], list(carry[2:])
            end = i32(-1)
            for k in range(4):
                first = jnp.maximum(rel, 2 * k)
                high = jnp.minimum(rel + WSEG, 2 * k + 2)
                given = jnp.minimum(lefts[k], jnp.maximum(high - first, 0))
                lefts[k] = lefts[k] - given
                low = first + given
                state = put(0, 0, slot, rel, profile, low, high, low != end, state)
                end = jnp.where(high > low, high, end)
            return (*state, *lefts)

        return lax.cond(jnp.logical_and(rel > -WSEG, rel < NSEG), covered, lambda c: c, carry)

    carry = lax.fori_loop(0, SLOTS, own_slot, (i32(0), i32(0), *(shares[k, me] for k in range(4))))
    state = carry[:2]
    for k in range(4):
        home = helped(place, k)
        share = shares[k, home]

        def lent_slot(slot, carry, k=k, home=home):
            rel, profile = window(home, slot)

            def covered(carry):
                for i in range(2):
                    row = NSEG + 2 * k + i
                    weights[row : row + 1] += padded[pl.ds(profile * 32 + 8 - rel + 2 * k + i, 1)]
                first = jnp.maximum(rel, 2 * k)
                taken = jnp.minimum(carry[2], jnp.maximum(jnp.minimum(rel + WSEG, 2 * k + 2) - first, 0))
                state = put(
                    SHARD + HALO + HALO * k, SHARD, SLOTS * (k + 1) + slot, rel, profile, first, first + taken,
                    True, carry[:2],
                )
                return (*state, carry[2] - taken)

            return lax.cond(jnp.logical_and(rel > -WSEG, rel < NSEG), covered, lambda c: c, carry)

        state = lax.fori_loop(0, jnp.where(share > 0, SLOTS, 0), lent_slot, (*state, share))[:2]
    rows, units = state
    unit[0, units] = rows + HALO

    for copy in loads:
        copy.wait()
    for half in range(2):
        part = head_weight[pl.ds(half * 128, 128)].astype(f32)
        head_turned[:, half * 128 : (half + 1) * 128] = part.T.astype(bf16)

    def batch(b, carry):
        begin, end = b * BATCH, jnp.minimum(b * BATCH + BATCH, units)
        shift = unit[0, begin] - HALO

        def fill(n, blanks):
            first = pl.multiple_of(unit[0, n] - shift, 32)
            norm, source = unit[4, n], pl.multiple_of(unit[3, n], 32)
            scale = norms[pl.ds(norm // SLOTS * 2 * SLOTS + norm % SLOTS, 1)]
            offset = norms[pl.ds(norm // SLOTS * 2 * SLOTS + SLOTS + norm % SLOTS, 1)]
            ahead = jnp.where(jnp.logical_and(n == begin, unit[5, n] == 0), 1, unit[5, n])

            def normalised(row, length):
                return (feats[pl.ds(row, length)].astype(f32) * scale + offset).astype(bf16)

            x_stack[pl.ds(first + HALO, SEG)] = normalised(pl.multiple_of(source + HALO, 32), SEG)

            @pl.when(ahead == 1)
            def _():
                x_stack[pl.ds(first, HALO)] = normalised(source, HALO)

            @pl.when(ahead == 2)
            def _():
                x_stack[pl.ds(first, HALO)] = jnp.zeros((HALO, 128), bf16)
                zeros[blanks] = first

            return blanks + jnp.where(ahead == 2, 1, 0)

        blanks = lax.fori_loop(begin, end, fill, i32(0))
        rows = unit[0, end - 1] - shift + SEG
        spans, first = [], i32(0)
        for size in SIZES:
            steps = (rows - first + (size - 1 if size == SIZES[-1] else 0)) // size
            spans.append((size, first, steps))
            first = first + steps * size
        run_batch(begin, end, shift, spans, blanks)
        return carry

    def run_batch(begin, end, shift, spans, blanks):
        def over_rows(body):
            for size, first, steps in spans:

                def step(index, carry, size=size, first=first):
                    body(pl.multiple_of(first + index * size, SIZES[-1]), size)
                    return carry

                lax.fori_loop(0, steps, step, 0)

        def layer(index, source, target, weight):
            spread = 2**index

            def body(first, length):
                block = source[pl.ds(first, length + HALO)]
                width, summed = block.shape[1], layer_bias[index : index + 1]
                shifted = [block[HALO - s * spread : HALO - s * spread + length] for s in (2, 1, 0)]
                if index == 0:
                    shifted = [jnp.concatenate(shifted[:2], axis=1), shifted[2]]
                start = 0
                for rows_of in shifted:
                    part = weight[start : start + rows_of.shape[1]]
                    start = start + rows_of.shape[1]
                    summed = summed + jnp.dot(rows_of, part, preferred_element_type=f32)
                made = gelu16(summed)
                if index:
                    made = made + block[HALO:]
                target[pl.ds(first + HALO, length)] = made

            over_rows(body)

            def blank(n, carry):
                target[pl.ds(pl.multiple_of(zeros[n], 32), HALO)] = jnp.zeros((HALO, 256), bf16)
                return carry

            if index < 3:
                lax.fori_loop(0, blanks, blank, 0)

        layer(0, x_stack, h_a, first_weight[...])
        layer(1, h_a, h_b, deep_weight[0])
        layer(2, h_b, h_a, deep_weight[1])
        layer(3, h_a, h_b, deep_weight[2])

        def gather(n, carry):
            for u in range(TOGETHER):
                index = begin + TOGETHER * n + u
                there = index < end
                index = jnp.where(there, index, begin)
                rows = pl.multiple_of(unit[0, index] - shift + HALO, 32)
                target = pl.ds(pl.multiple_of(unit[1, index], SEG), SEG)
                weight = padded[pl.ds(jnp.where(there, unit[2, index], 0), 1)]
                made = lax.dot_general(
                    head_turned[...], h_b[pl.ds(rows, SEG)], (((1,), (1,)), ((), ())), preferred_element_type=f32
                )
                total[:, target] += made * weight
            return carry

        lax.fori_loop(0, (end - begin + TOGETHER - 1) // TOGETHER, gather, 0)

    lax.fori_loop(0, (units + BATCH - 1) // BATCH, batch, 0)

    bias = jnp.broadcast_to(head_bias[...], (8, 128)).T[:, :1]

    scale = 1.0 / jnp.maximum(weights[...], 1.0)
    for k in range(NSEG):
        made = total[:, k * SEG : (k + 1) * SEG] + bias * weights[k : k + 1]
        sums[pl.ds(k * SEG, SEG)] = (made * scale[k : k + 1]).astype(bf16).T
        lent = total[:, SHARD + k * SEG : SHARD + (k + 1) * SEG] * scale[NSEG + k : NSEG + k + 1]
        lent_sums[pl.ds(k * SEG, SEG)] = lent.astype(bf16).T


def run_network(count, table, shares, feats, lent, norms, lent_norms, net, profiles):
    vmem, smem, hbm = (pl.BlockSpec(memory_space=m) for m in (pltpu.VMEM, pltpu.SMEM, pl.ANY))
    first_weight, deep_weight, layer_bias, head_weight, head_bias = net
    return pl.pallas_call(
        functools.partial(network_kernel, count),
        out_shape=[
            jax.ShapeDtypeStruct((SHARD, 128), bf16),
            jax.ShapeDtypeStruct((SHARD, 128), bf16),
        ],
        in_specs=[smem, smem, hbm, hbm, hbm, hbm, hbm, hbm, vmem, hbm, vmem, vmem],
        out_specs=[vmem, vmem],
        scratch_shapes=[
            pltpu.VMEM((SHARD + HALO + 4 * (512 + HALO), 128), bf16),
            pltpu.VMEM((10 * SLOTS, 128), f32),
            pltpu.VMEM((384, 256), bf16),
            pltpu.VMEM((3, 768, 256), bf16),
            pltpu.VMEM((256, 128), bf16),
            pltpu.VMEM((CAPACITY + HALO, 128), bf16),
            pltpu.VMEM((CAPACITY + HALO, 256), bf16),
            pltpu.VMEM((CAPACITY + HALO, 256), bf16),
            pltpu.VMEM((128, 2 * SHARD), f32),
            pltpu.VMEM((128, 256), bf16),
            pltpu.VMEM((4 * 32, SEG), f32),
            pltpu.VMEM((2 * NSEG, SEG), f32),
            pltpu.SMEM((6, UNITS), i32),
            pltpu.SMEM((BATCH,), i32),
            pltpu.SemaphoreType.DMA((13,)),
        ],
        compiler_params=pltpu.CompilerParams(vmem_limit_bytes=62 * 2**20),
    )(table, shares, feats, lent, norms, lent_norms, first_weight, deep_weight, layer_bias, head_weight, head_bias, profiles)


def return_kernel(lent_sums, arrived, send_sem, recv_sem):
    me = lax.axis_index("tm")
    place = coordinates(me)
    barrier = pltpu.get_barrier_semaphore()
    for k in range(4):
        for partner in (helper(place, k), helped(place, k)):
            pl.semaphore_signal(barrier, inc=1, device_id=(partner,), device_id_type=MESH)
    pl.semaphore_wait(barrier, 8)
    copies = []
    for k in range(4):
        rows = pl.ds(512 * k, 512)
        copy = pltpu.make_async_remote_copy(
            src_ref=lent_sums.at[rows], dst_ref=arrived.at[rows], send_sem=send_sem.at[k], recv_sem=recv_sem.at[k],
            device_id=(helped(place, k),), device_id_type=MESH,
        )
        copy.start()
        copies.append(copy)
    for copy in copies:
        copy.wait()


def bring_back(lent_sums):
    hbm = pl.BlockSpec(memory_space=pl.ANY)
    return pl.pallas_call(
        return_kernel,
        out_shape=jax.ShapeDtypeStruct((SHARD, 128), bf16),
        in_specs=[hbm],
        out_specs=hbm,
        scratch_shapes=[pltpu.SemaphoreType.DMA((4,)), pltpu.SemaphoreType.DMA((4,))],
        compiler_params=pltpu.CompilerParams(
            collective_id=1, has_side_effects=True, vmem_limit_bytes=56 * 2**20
        ),
    )(lent_sums)


def per_device(
    stream, stem_weight, stem_bias, first_weight, deep_weight, layer_bias, head_weight, head_bias,
    profiles, starts, profile_index, counts,
):
    count = lax.axis_size("tm")
    feats, norms, table, shares, lent, lent_norms = make_features(
        count, starts, profile_index, counts, stream, stem_weight.reshape(7 * 128, 128), stem_bias.reshape(1, 128)
    )
    net = (
        first_weight.reshape(3 * 128, 256),
        deep_weight.reshape(3, 3 * 256, 256),
        layer_bias,
        head_weight,
        head_bias.reshape(1, 128),
    )
    sums, lent_sums = run_network(count, table, shares, feats, lent, norms, lent_norms, net, profiles)
    return (sums.astype(f32) + bring_back(lent_sums).astype(f32)).astype(bf16)


def solution(mesh):
    in_specs = (P("tm", None), P(), P(), P(), P(), P(), P(), P(), P(), P("tm"), P("tm"), P("tm"))
    return jax.shard_map(
        per_device, mesh=mesh, in_specs=in_specs, out_specs=P("tm", None), check_vma=False
    )
```
